256 devices in a mesh: band: 16 (over z, x_lo), patch: 16 (over x_hi, y, core).
Axes of the slice: x: 4 (x_hi: 2, x_lo: 2; x = x_hi * 2 + x_lo), y: 4, z: 8, core: 2. Of those that a mesh axis runs over, the one named last changes fastest.
Arguments:
- latents: bfloat16 [16, 40960, 512], P('band', 'patch'), may hold values from -6 to 6
- owners: int32 [16], replicated, may hold values from 0 to 15, as said below
- block_rows: int32 [16, 128], replicated, may hold values from 0 to 2559
- interp_weights: bfloat16 [16, 4096, 128], P('band', 'patch'), may hold values from -0.5 to 0.5
- w_first: bfloat16 [16, 512, 512], P('band'), may hold values from -0.25 to 0.25
- b_first: float32 [16, 512], P('band'), may hold values from -3 to 3
- w_second: bfloat16 [16, 512, 512], P('band'), may hold values from -0.25 to 0.25
- b_second: float32 [16, 512], P('band'), may hold values from -4 to 4
- gain: float32 [16, 512], P('band'), may hold values from 0.1 to 1.9
- w_out: bfloat16 [16, 12, 512], P('band'), may hold values from -0.25 to 0.25
- b_out: float32 [16, 12], P('band'), may hold values from -4 to 4
Outputs:
- grid_fields: float32 [16, 12, 65536], P('band', None, 'patch')
The draws below stay inside these ranges and needn't reach their ends.
Inputs may be any that keep to these rules, and one draw needn't show every extreme that they name: `owners`: no patch owns more than 4 tiles, and one patch owns exactly 4.
All inputs are finite; a program needn't handle non-finite values.
Results may differ from the reference program's by a relative error of at most 0.003.
Values may be sent and summed in bfloat16 or wider, within the bound.
No kernel may reach another device: no remote copies, remote signals or barrier semaphores. Data moves between devices by JAX's collectives and lax.ppermute only.
A program may use at most 64 MiB of HBM per device.

```python
import jax
import jax.numpy as jnp
from jax import lax

D = 512
BLK = 128
TILES = 16
MESH_DEV = 2560
CH = 12
CAP = 4
CELLS_T = 4096
MESH = 40960
BANDS = 16
N_PATCH = 16


def draw_owners(key, part):
    key_heavy, key_order, key_offset = jax.random.split(jax.random.fold_in(key, 11), 3)
    heavy_owner = jax.random.randint(key_heavy, (), 0, N_PATCH)
    tile_order = jax.random.permutation(key_order, TILES)
    offset_draw = jax.random.randint(key_offset, (), 0, N_PATCH - 1)
    position = jnp.arange(TILES)
    others = (heavy_owner + 1 + (position - CAP + offset_draw) % (N_PATCH - 1)) % N_PATCH
    owner_by_position = jnp.where(position < CAP, heavy_owner, others).astype(jnp.int32)
    return jnp.zeros((TILES,), jnp.int32).at[tile_order].set(owner_by_position)


def place_ends(drawn, own_key, smallest, high):
    extent = drawn.shape
    spot = [jax.random.randint(jax.random.fold_in(own_key, axis), (), 0, extent[axis]) for axis in range(len(extent))]
    drawn = drawn.at[tuple(spot)].set(smallest)
    longest = extent.index(max(extent))
    spot[longest] = (spot[longest] + 1) % extent[longest]
    return drawn.at[tuple(spot)].set(high)


def steps_of(own_key, shape, pieces, low, top_value):
    loudness = 1.0
    for axis_at, shards_of in pieces:
        steps = jax.random.uniform(jax.random.fold_in(jax.random.fold_in(own_key, 6), axis_at), (shards_of,), jnp.float32, low / len(pieces), top_value / len(pieces))
        loudness = loudness * jnp.repeat(jnp.exp(steps), shape[axis_at] // shards_of).reshape((-1,) + (1,) * (len(shape) - 1 - axis_at))
    return loudness


def noise(own_key, extent, spread, limit, pieces=(), kind=jnp.bfloat16):
    array = spread * jax.random.normal(own_key, extent, jnp.float32)
    if pieces:
        array = array * steps_of(own_key, extent, pieces, -0.22, 0.18)
    return jnp.clip(array, -limit, limit).astype(kind)


def setup_inputs(seed: int = 0) -> dict:
    keys = jax.random.split(jax.random.key(seed), 12)
    latents = noise(keys[0], (BANDS, MESH, D), 1.0, 6.0, ((0, 16), (1, 16)))
    owners = draw_owners(jax.random.fold_in(keys[11], 71), 0)
    block_rows = place_ends(jax.random.randint(keys[2], (TILES, BLK), 0, MESH_DEV), jax.random.fold_in(keys[2], 1), 0, MESH_DEV - 1).astype(jnp.int32)
    interp_weights = noise(keys[3], (TILES, CELLS_T, BLK), BLK ** -0.5, 0.5, ((0, 16), (1, 16)))
    w_first = noise(keys[4], (BANDS, D, D), D ** -0.5, 0.25, ((0, 16),))
    b_first = noise(keys[5], (BANDS, D), 0.5, 3.0, ((0, 16),), jnp.float32)
    w_second = noise(keys[6], (BANDS, D, D), D ** -0.5, 0.25, ((0, 16),))
    b_second = noise(keys[7], (BANDS, D), 1.0, 4.0, ((0, 16),), jnp.float32)
    gain = jnp.clip(1.0 + 0.18 * jax.random.normal(keys[8], (BANDS, D), jnp.float32), 0.1, 1.9)
    w_out = noise(keys[9], (BANDS, CH, D), D ** -0.5, 0.25, ((0, 16),))
    b_out = noise(keys[10], (BANDS, CH), 1.0, 4.0, ((0, 16),), jnp.float32)
    return {"latents": latents, "owners": owners, "block_rows": block_rows, "interp_weights": interp_weights, "w_first": w_first, "b_first": b_first, "w_second": w_second, "b_second": b_second, "gain": gain, "w_out": w_out, "b_out": b_out}


def decode_rows(interp, w_first, b_first, w_second, b_second, gain, w_out, b_out):
    hidden = jax.nn.silu(jnp.dot(interp, w_first, preferred_element_type=jnp.float32) + b_first).astype(jnp.bfloat16)
    second = jnp.dot(hidden, w_second, preferred_element_type=jnp.float32) + b_second
    mean_value = lax.optimization_barrier(jnp.mean(second, axis=-1, keepdims=True))
    centred = second - mean_value
    variance = lax.optimization_barrier(jnp.mean(centred * centred, axis=-1, keepdims=True))
    normed = (centred * lax.rsqrt(variance + 1e-05) * gain).astype(jnp.bfloat16)
    result = lax.dot_general(w_out, normed, (((1,), (1,)), ((), ())), preferred_element_type=jnp.float32)
    return result + b_out[:, None]

def reference(latents, owners, block_rows, interp_weights, w_first, b_first, w_second, b_second, gain, w_out, b_out):
    mesh_dev = latents.shape[1] // N_PATCH

    def one_band(band_args):
        band_latents, first_w, first_b, second_w, second_b, band_gain, out_w, out_b = band_args

        def one_tile(tile_index):
            rows_global = owners[tile_index] * mesh_dev + block_rows[tile_index]
            block = jnp.take(band_latents, rows_global.astype(jnp.int32), axis=0)
            interp = jnp.dot(interp_weights[tile_index], block, preferred_element_type=jnp.float32).astype(jnp.bfloat16)
            return decode_rows(interp, first_w, first_b, second_w, second_b, band_gain, out_w, out_b)
        per_tile = lax.map(one_tile, jnp.arange(TILES, dtype=jnp.int32))
        return jnp.transpose(per_tile, (1, 0, 2)).reshape(per_tile.shape[1], -1)
    return lax.map(one_band, (latents, w_first, b_first, w_second, b_second, gain, w_out, b_out))
```

```python
import jax
import jax.numpy as jnp
from jax import lax
from jax.experimental import pallas as pl
from jax.experimental.pallas import tpu as pltpu
from jax.sharding import PartitionSpec as P

ZS = 8
DY_CORE = {0: (2, 0), 1: (2, 1), 2: (1, 0), 3: (1, 1), 7: (3, 0), 6: (3, 1), 5: (0, 0), 4: (0, 1)}
DZ_OF = {pair: dz for dz, pair in DY_CORE.items()}


def joint(z, x_lo, x_hi, y, core):
    return (z * 2 + x_lo) * 16 + x_hi * 8 + y * 2 + core


def scatter_pairs(flip):
    pairs = []
    for tile in range(16):
        z_t, core_t = tile // 2, tile % 2
        xh_t, y_t = tile // 8, (tile // 2) % 4
        for xh in range(2):
            for y in range(4):
                for core in range(2):
                    dz = DZ_OF[((y - y_t) % 4, core)]
                    side = (core_t + (xh != xh_t) + flip) % 2
                    pairs.append(
                        (
                            joint(z_t, core_t, xh, y, core),
                            joint((z_t + dz) % ZS, side, xh_t, y_t, core_t),
                        )
                    )
    return pairs


def along_z(shift):
    return [(b, ((b // 2 + shift) % ZS) * 2 + b % 2) for b in range(16)]


def to_chip(dx, dy):
    return [
        (p, ((p // 8) ^ dx) * 8 + (((p // 2) % 4 + dy) % 4) * 2 + p % 2) for p in range(16)
    ]


CHIP_OFFSETS = [(dx, dy) for dx in range(2) for dy in range(4)]
VMEM_LIMIT = 48 * 1024 * 1024


def rank_of(owners, tile):
    def step(i, rank):
        return rank + ((i < tile) & (owners[i] == owners[tile])).astype(jnp.int32)

    return lax.fori_loop(0, 16, step, jnp.int32(0))


def gather_kernel(owners, rows_ref, latents_ref, out_ref):
    me = lax.axis_index("patch")
    row_id = lax.broadcasted_iota(jnp.int32, (128, 128), 0)
    col_id = lax.broadcasted_iota(jnp.int32, (128, 128), 1)

    def find(i, carry):
        count, tiles = carry
        mine = owners[i] == me
        tiles = tuple(jnp.where(mine & (count == s), i, tiles[s]) for s in range(4))
        return count + mine.astype(jnp.int32), tiles

    _, tiles = lax.fori_loop(0, 16, find, (jnp.int32(0), (jnp.int32(0),) * 4))
    lane = lax.broadcasted_iota(jnp.int32, (128, 2560), 1)
    for s in range(4):
        rows = rows_ref[pl.ds(tiles[s], 1), :]
        column = jnp.sum(jnp.where(row_id == col_id, rows, 0), axis=1, keepdims=True)
        chosen = (lane == column).astype(jnp.float32).astype(jnp.bfloat16)
        out_ref[s * 128 : (s + 1) * 128, :] = jnp.dot(
            chosen, latents_ref[...], preferred_element_type=jnp.float32
        ).astype(jnp.bfloat16)


def gather_rows(owners, block_rows, latents):
    return pl.pallas_call(
        gather_kernel,
        out_shape=jax.ShapeDtypeStruct((512, 512), jnp.bfloat16),
        in_specs=[
            pl.BlockSpec(memory_space=pltpu.SMEM),
            pl.BlockSpec(memory_space=pltpu.VMEM),
            pl.BlockSpec(memory_space=pltpu.VMEM),
        ],
        out_specs=pl.BlockSpec(memory_space=pltpu.VMEM),
        compiler_params=pltpu.CompilerParams(vmem_limit_bytes=VMEM_LIMIT),
        name="gather_rows",
    )(owners, block_rows, latents)


def pack_kernel(owners, mine_ref, other_ref, *out_refs):
    me = lax.axis_index("patch")
    chip, core = me // 2, me % 2
    for (dx, dy), out_ref in zip(CHIP_OFFSETS, out_refs):
        tile = ((me // 8) ^ dx) * 8 + ((chip % 4 + dy) % 4) * 2 + core
        owner = owners[tile]
        here = owner // 2 == chip
        start = pl.multiple_of(jnp.where(here, rank_of(owners, tile), 0) % 4 * 128, 128)
        own = owner % 2 == core

        @pl.when(own)
        def _():
            out_ref[...] = mine_ref[pl.ds(start, 128), :]

        @pl.when(jnp.logical_not(own))
        def _():
            out_ref[...] = other_ref[pl.ds(start, 128), :]


def pack_blocks(owners, mine, other):
    vmem = pl.BlockSpec(memory_space=pltpu.VMEM)
    return pl.pallas_call(
        pack_kernel,
        out_shape=[jax.ShapeDtypeStruct((128, 512), jnp.bfloat16)] * 8,
        in_specs=[pl.BlockSpec(memory_space=pltpu.SMEM), vmem, vmem],
        out_specs=[vmem] * 8,
        name="pack_blocks",
    )(owners, mine, other)


def split(value):
    high = value.astype(jnp.bfloat16)
    return high, (value - high.astype(jnp.float32)).astype(jnp.bfloat16)


def prepare_kernel(w2_ref, b2_ref, gain_ref, w_out_ref, b_out_ref, head_ref, b2c_ref, shift_ref):
    w2 = w2_ref[...]
    gw = gain_ref[...] * w_out_ref[...].astype(jnp.float32)
    gw = jnp.concatenate([gw, jnp.zeros((4, 512), jnp.float32)], axis=0)
    g1 = gw.astype(jnp.bfloat16)
    g2, g3 = split(gw - g1.astype(jnp.float32))
    ones = jnp.ones((8, 512), jnp.bfloat16)
    stacked = jnp.concatenate([g1, g2, g3, ones, ones], axis=0)
    contract = (((1,), (1,)), ((), ()))
    raw = lax.dot_general(stacked, w2, contract, preferred_element_type=jnp.float32)
    w2_mean = raw[48:49] * (1.0 / 512)
    total = jnp.sum(gw, axis=1, keepdims=True)
    head = raw[0:16] + raw[16:32] + raw[32:48] - total * w2_mean
    high, low = split(head)
    mean_high, mean_low = split(jnp.broadcast_to(w2_mean, (16, 512)))
    pad = jnp.zeros((64, 512), jnp.bfloat16)
    rows = jnp.concatenate([high, low, mean_high, mean_low, pad], axis=0)
    head_ref[...] = rows
    b2 = b2_ref[...]
    b2c = b2 - jnp.mean(b2, axis=1, keepdims=True)
    b2c_ref[...] = b2c
    shift = jnp.sum(gw * b2c, axis=1, keepdims=True)
    shift_ref[...] = jnp.concatenate(
        [
            jnp.broadcast_to(shift, (16, 128)),
            jnp.broadcast_to(b_out_ref[...], (16, 128)),
        ],
        axis=0,
    )


def prepare(w2, b2, gain, w_out, b_out):
    vmem = pl.BlockSpec(memory_space=pltpu.VMEM)
    return pl.pallas_call(
        prepare_kernel,
        out_shape=[
            jax.ShapeDtypeStruct((128, 512), jnp.bfloat16),
            jax.ShapeDtypeStruct((1, 512), jnp.float32),
            jax.ShapeDtypeStruct((32, 128), jnp.float32),
        ],
        in_specs=[vmem] * 5,
        out_specs=[vmem] * 3,
        name="prepare",
    )(w2, b2, gain, w_out, b_out)


def chunk_pair(z, x_lo, tile):
    z_t, core_t = tile // 2, tile % 2
    xh_t, y_t = tile // 8, (tile // 2) % 4
    dz = (z - z_t + ZS) % ZS
    dy = jnp.int32(0)
    core = jnp.int32(0)
    for key, (dy_k, core_k) in DY_CORE.items():
        dy = jnp.where(dz == key, dy_k, dy)
        core = jnp.where(dz == key, core_k, core)
    y = (y_t + dy) % 4
    near = xh_t * 8 + y * 2 + core
    far = (1 - xh_t) * 8 + y * 2 + core
    same = x_lo == core_t
    return jnp.where(same, near, far), jnp.where(same, far, near)


def decode_kernel(offsets, owners, *refs):
    count = len(offsets)
    piece_refs = refs[:count]
    block_refs = refs[count : count + 8]
    w1_ref, b1_ref, w2_ref, head_ref, b2c_ref, shift_ref, out_ref, block, m_ref = refs[count + 8 :]
    band = lax.axis_index("band")
    tile = lax.axis_index("patch")
    owner_chip = owners[tile] // 2
    chip = tile // 2
    which = (owner_chip // 4 ^ chip // 4) * 4 + (chip % 4 - owner_chip % 4 + 4) % 4
    for k in range(8):

        @pl.when(which == k)
        def _():
            block[...] = block_refs[k][...]

    m = 0.5 * jnp.dot(block[...], w1_ref[...], preferred_element_type=jnp.float32)
    high, low = split(m)
    m_ref[0:128, :] = high
    m_ref[128:256, :] = low
    half_b1 = 0.5 * b1_ref[...]
    contract = (((1,), (1,)), ((), ()))
    for piece_ref, offset in zip(piece_refs, offsets):
        chunks = chunk_pair((band // 2 + offset + ZS) % ZS, band % 2, tile)
        for part in range(2):
            weights = piece_ref[part * 256 : (part + 1) * 256, :]
            both = jnp.concatenate([weights, weights], axis=1)
            half = jnp.dot(both, m_ref[...], preferred_element_type=jnp.float32) + half_b1
            hidden = (half + half * jnp.tanh(half)).astype(jnp.bfloat16)
            second = jnp.dot(hidden, w2_ref[...], preferred_element_type=jnp.float32)
            headed = lax.dot_general(
                hidden, head_ref[...], contract, preferred_element_type=jnp.float32
            )
            mean = headed[:, 32:33] + headed[:, 48:49]
            centred = second + b2c_ref[...] - mean
            variance = jnp.mean(centred * centred, axis=1, keepdims=True)
            scale = lax.rsqrt(variance + 1e-05)
            lane = lax.broadcasted_iota(jnp.int32, (256, 128), 1)
            flipped = jnp.where(lane == 64, scale, headed).T
            fields = flipped[0:16] + flipped[16:32] + shift_ref[0:16, 0:1]
            fields = fields * flipped[64:65] + shift_ref[16:32, 0:1]
            start = pl.multiple_of(chunks[part] * 256, 256)
            out_ref[:, pl.ds(start, 256)] = fields[0:12]


def decode(offsets, pieces, blocks, owners, w1, b1, w2, head, b2c, shift):
    vmem = pl.BlockSpec(memory_space=pltpu.VMEM)
    count = len(pieces)
    return pl.pallas_call(
        lambda *refs: decode_kernel(offsets, *refs),
        out_shape=jax.ShapeDtypeStruct((12, 4096), jnp.float32),
        in_specs=[pl.BlockSpec(memory_space=pltpu.SMEM)] + [vmem] * (count + 8 + 6),
        out_specs=vmem,
        scratch_shapes=[
            pltpu.VMEM((128, 512), jnp.bfloat16),
            pltpu.VMEM((256, 512), jnp.bfloat16),
        ],
        compiler_params=pltpu.CompilerParams(vmem_limit_bytes=VMEM_LIMIT),
        name="decode",
    )(owners, *pieces, *blocks, w1, b1, w2, head, b2c, shift)


def body(
    latents, owners, block_rows, interp_weights, w_first, b_first, w_second, b_second, gain,
    w_out, b_out,
):
    weights = interp_weights[0]
    first = lax.ppermute(weights, ("band", "patch"), scatter_pairs(0))
    other = lax.ppermute(weights, ("band", "patch"), scatter_pairs(1))
    slots = gather_rows(owners, block_rows, latents[0])
    neighbour = lax.ppermute(slots, "patch", [(p, p ^ 1) for p in range(16)])
    packed = pack_blocks(owners, slots, neighbour)
    blocks = [packed[0]] + [
        lax.ppermute(packed[k], "patch", to_chip(*CHIP_OFFSETS[k])) for k in range(1, 8)
    ]
    head, b2c, shift = prepare(
        w_second[0], b_second, gain, w_out[0],
        jnp.pad(b_out[0], (0, 4))[:, None],
    )
    own = jnp.concatenate([first, other], axis=0)
    up, down = [own], [own]
    for _ in range(3):
        up.append(lax.ppermute(up[-1], "band", along_z(1)))
        down.append(lax.ppermute(down[-1], "band", along_z(-1)))
    last = jnp.concatenate(
        [
            lax.ppermute(up[3][:256], "band", along_z(1)),
            lax.ppermute(down[3][256:], "band", along_z(-1)),
        ],
        axis=0,
    )
    pieces = [own, up[1], down[1], up[2], down[2], up[3], down[3], last]
    offsets = [0, -1, 1, -2, 2, -3, 3, 4]
    fields = decode(
        offsets, pieces, blocks, owners, w_first[0], b_first, w_second[0], head, b2c, shift
    )
    return fields[None]


def solution(mesh):
    return jax.shard_map(
        body,
        mesh=mesh,
        in_specs=(
            P("band", "patch", None),
            P(),
            P(),
            P("band", "patch", None),
            P("band", None, None),
            P("band", None),
            P("band", None, None),
            P("band", None),
            P("band", None),
            P("band", None, None),
            P("band", None),
        ),
        out_specs=P("band", None, "patch"),
        check_vma=False,
    )
```

```python
import jax
import jax.numpy as jnp
from jax import lax
from jax.experimental import pallas as pl
from jax.experimental.pallas import tpu as pltpu
from jax.sharding import PartitionSpec as P

ZS = 8
DY_CORE = {0: (2, 0), 1: (2, 1), 2: (1, 0), 3: (1, 1), 7: (3, 0), 6: (3, 1), 5: (0, 0), 4: (0, 1)}
DZ_OF = {pair: dz for dz, pair in DY_CORE.items()}


def joint(z, x_lo, x_hi, y, core):
    return (z * 2 + x_lo) * 16 + x_hi * 8 + y * 2 + core


def scatter_pairs(flip):
    pairs = []
    for tile in range(16):
        z_t, core_t = tile // 2, tile % 2
        xh_t, y_t = tile // 8, (tile // 2) % 4
        for xh in range(2):
            for y in range(4):
                for core in range(2):
                    dz = DZ_OF[((y - y_t) % 4, core)]
                    side = (core_t + (xh != xh_t) + flip) % 2
                    pairs.append(
                        (
                            joint(z_t, core_t, xh, y, core),
                            joint((z_t + dz) % ZS, side, xh_t, y_t, core_t),
                        )
                    )
    return pairs


def along_z(shift):
    return [(b, ((b // 2 + shift) % ZS) * 2 + b % 2) for b in range(16)]


def to_chip(dx, dy):
    return [
        (p, ((p // 8) ^ dx) * 8 + (((p // 2) % 4 + dy) % 4) * 2 + p % 2) for p in range(16)
    ]


VMEM = pl.BlockSpec(memory_space=pltpu.VMEM)
HBM = pl.BlockSpec(memory_space=pltpu.HBM)
WIDE = pltpu.CompilerParams(vmem_limit_bytes=56 * 1024 * 1024)
PARAMS = pltpu.CompilerParams(vmem_limit_bytes=8 * 1024 * 1024)
CONTRACT_LANES = (((1,), (1,)), ((), ()))


def start_loads(pairs, sems):
    loads = [
        pltpu.make_async_copy(source, target, sems.at[i])
        for i, (source, target) in enumerate(pairs)
    ]
    for load in loads:
        load.start()
    return loads


def split(value):
    high = value.astype(jnp.bfloat16)
    return high, (value - high.astype(jnp.float32)).astype(jnp.bfloat16)


def gather_kernel(
    owners_hbm, rows_hbm, latents_hbm, b1_hbm, b2_hbm, gain_hbm, w_out_hbm, b_out_hbm,
    mine_hbm, other_hbm, vectors_hbm,
    owners, rows_ref, latents_ref, chosen_ref, mine_ref, other_ref,
    b1_ref, b2_ref, gain_ref, w_out_ref, b_out_ref, vectors_ref, sems,
):
    loads = start_loads(
        [
            (owners_hbm, owners),
            (rows_hbm, rows_ref),
            (latents_hbm.at[0], latents_ref),
            (b1_hbm, b1_ref),
            (b2_hbm, b2_ref),
            (gain_hbm, gain_ref),
            (w_out_hbm.at[0], w_out_ref),
            (b_out_hbm, b_out_ref),
        ],
        sems,
    )
    mine_ref[...] = jnp.zeros_like(mine_ref)
    other_ref[...] = jnp.zeros_like(other_ref)
    me = lax.axis_index("patch")
    row_id = lax.broadcasted_iota(jnp.int32, (128, 128), 0)
    col_id = lax.broadcasted_iota(jnp.int32, (128, 128), 1)
    lane = lax.broadcasted_iota(jnp.int32, (128, 2560), 1)
    loads[0].wait()
    loads[1].wait()

    def find(i, carry):
        count, tiles = carry
        mine = owners[i] == me
        tiles = tuple(jnp.where(mine & (count == s), i, tiles[s]) for s in range(4))
        return count + mine.astype(jnp.int32), tiles

    count, tiles = lax.fori_loop(0, 16, find, (jnp.int32(0), (jnp.int32(0),) * 4), unroll=True)
    for s in range(4):

        @pl.when(s < count)
        def _():
            rows = rows_ref[pl.ds(tiles[s], 1), :]
            column = jnp.sum(jnp.where(row_id == col_id, rows, 0), axis=1, keepdims=True)
            chosen_ref[s * 128 : (s + 1) * 128, :] = (
                (lane == column).astype(jnp.float32).astype(jnp.bfloat16)
            )

    loads[2].wait()
    for s in range(4):

        @pl.when(s < count)
        def _():
            block = jnp.dot(
                chosen_ref[s * 128 : (s + 1) * 128, :],
                latents_ref[...],
                preferred_element_type=jnp.float32,
            ).astype(jnp.bfloat16)
            chip = tiles[s] // 2
            here = tiles[s] % 2 == me % 2

            @pl.when(here)
            def _():
                mine_ref[chip] = block

            @pl.when(jnp.logical_not(here))
            def _():
                other_ref[chip] = block

    stores = start_loads([(other_ref, other_hbm), (mine_ref, mine_hbm)], sems)
    for load in loads[3:]:
        load.wait()
    row_id = lax.broadcasted_iota(jnp.int32, (16, 12), 0)
    col_id = lax.broadcasted_iota(jnp.int32, (16, 12), 1)
    b_out = jnp.sum(jnp.where(row_id == col_id, b_out_ref[...], 0.0), axis=1, keepdims=True)
    vectors_ref[0:8, :] = jnp.broadcast_to(0.5 * b1_ref[...], (8, 512))
    vectors_ref[8:16, :] = jnp.broadcast_to(b2_ref[...], (8, 512))
    vectors_ref[16:28, :] = gain_ref[...] * w_out_ref[...].astype(jnp.float32)
    vectors_ref[28:32, :] = jnp.zeros((4, 512), jnp.float32)
    vectors_ref[32:48, :] = jnp.broadcast_to(b_out, (16, 512))
    stores += start_loads([(vectors_ref, vectors_hbm)], sems.at[pl.ds(2, 1)])
    for store in stores:
        store.wait()


VECTORS = ((48, 512), jnp.float32)


def gather_rows(owners, block_rows, latents, b1, b2, gain, w_out, b_out):
    blocks = jax.ShapeDtypeStruct((8, 128, 512), jnp.bfloat16)
    row = pltpu.VMEM((1, 512), jnp.float32)
    return pl.pallas_call(
        gather_kernel,
        out_shape=[blocks, blocks, jax.ShapeDtypeStruct(*VECTORS)],
        in_specs=[HBM] * 8,
        out_specs=[HBM] * 3,
        scratch_shapes=[
            pltpu.SMEM((16,), jnp.int32),
            pltpu.VMEM((16, 128), jnp.int32),
            pltpu.VMEM((2560, 512), jnp.bfloat16),
            pltpu.VMEM((512, 2560), jnp.bfloat16),
            pltpu.VMEM((8, 128, 512), jnp.bfloat16),
            pltpu.VMEM((8, 128, 512), jnp.bfloat16),
            row,
            row,
            row,
            pltpu.VMEM((12, 512), jnp.bfloat16),
            pltpu.VMEM((1, 12), jnp.float32),
            pltpu.VMEM(*VECTORS),
            pltpu.SemaphoreType.DMA((8,)),
        ],
        compiler_params=WIDE,
        name="gather_rows",
    )(owners, block_rows, latents, b1, b2, gain, w_out, b_out)


def prepare_kernel(w1_ref, w2_ref, vectors_ref, w1_out, w2_out, head_ref, small_ref):
    gw = vectors_ref[16:32, :]
    g1 = gw.astype(jnp.bfloat16)
    g2, g3 = split(gw - g1.astype(jnp.float32))
    ones = jnp.ones((16, 512), jnp.bfloat16)
    stacked = jnp.concatenate([g1, g2, g3, ones], axis=0)
    raw = lax.dot_general(stacked, w2_ref[0], CONTRACT_LANES, preferred_element_type=jnp.float32)
    w2_mean = raw[48:49] * (1.0 / 512)
    total = jnp.sum(gw, axis=1, keepdims=True)
    head = raw[0:16] + raw[16:32] + raw[32:48] - total * w2_mean
    high, low = split(head)
    mean_high, mean_low = split(jnp.broadcast_to(w2_mean, (16, 512)))
    pad = jnp.zeros((64, 512), jnp.bfloat16)
    head_ref[...] = jnp.concatenate([high, low, mean_high, mean_low, pad], axis=0)
    b2 = vectors_ref[8:9, :]
    b2c = b2 - jnp.mean(b2, axis=1, keepdims=True)
    shift = jnp.sum(gw * b2c, axis=1, keepdims=True)
    small_ref[0:8, :] = jnp.broadcast_to(b2c, (8, 512))
    small_ref[8:16, :] = vectors_ref[0:8, :]
    small_ref[16:32, :] = jnp.broadcast_to(shift, (16, 512))
    small_ref[32:48, :] = vectors_ref[32:48, :]
    w1_out[...] = w1_ref[0]
    w2_out[...] = w2_ref[0]


def prepare(w1, w2, vectors):
    square = jax.ShapeDtypeStruct((512, 512), jnp.bfloat16)
    return pl.pallas_call(
        prepare_kernel,
        out_shape=[
            square,
            square,
            jax.ShapeDtypeStruct((128, 512), jnp.bfloat16),
            jax.ShapeDtypeStruct(*VECTORS),
        ],
        in_specs=[VMEM] * 3,
        out_specs=[VMEM] * 4,
        compiler_params=PARAMS,
        cost_estimate=pl.CostEstimate(
            flops=2 * 64 * 512 * 512, bytes_accessed=4 * 1024 * 1024, transcendentals=0
        ),
        name="prepare",
    )(w1, w2, vectors)


def join_kernel(near_ref, far_ref, own_ref):
    own_ref[0:256, :] = near_ref[...]
    own_ref[256:512, :] = far_ref[...]


def join(near, far):
    return pl.pallas_call(
        join_kernel,
        out_shape=jax.ShapeDtypeStruct((512, 128), jnp.bfloat16),
        in_specs=[VMEM] * 2,
        out_specs=VMEM,
        compiler_params=PARAMS,
        name="join",
    )(near, far)


def pack_kernel(mine_ref, other_ref, blocks_ref):
    blocks_ref[...] = mine_ref[...] + other_ref[...]


def pack(mine, other):
    return pl.pallas_call(
        pack_kernel,
        out_shape=jax.ShapeDtypeStruct((8, 128, 512), jnp.bfloat16),
        in_specs=[VMEM] * 2,
        out_specs=VMEM,
        compiler_params=PARAMS,
        name="pack",
    )(mine, other)


def chunk_pair(z, x_lo, tile):
    z_t, core_t = tile // 2, tile % 2
    xh_t, y_t = tile // 8, (tile // 2) % 4
    dz = (z - z_t + ZS) % ZS
    dy = jnp.int32(0)
    core = jnp.int32(0)
    for key, (dy_k, core_k) in DY_CORE.items():
        dy = jnp.where(dz == key, dy_k, dy)
        core = jnp.where(dz == key, core_k, core)
    y = (y_t + dy) % 4
    near = xh_t * 8 + y * 2 + core
    far = (1 - xh_t) * 8 + y * 2 + core
    same = x_lo == core_t
    return jnp.where(same, near, far), jnp.where(same, far, near)


def decode_pieces(pieces, offsets, m_ref, w2_ref, head_ref, small_ref, out_hbm, staged, sems):
    band = lax.axis_index("band")
    tile = lax.axis_index("patch")
    lane = lax.broadcasted_iota(jnp.int32, (256, 128), 1)
    b2c = small_ref[0:1, :]
    half_b1 = small_ref[8:9, :]
    shift = small_ref[16:32, 0:1]
    b_out = small_ref[32:48, 0:1]
    copies = []
    for index, (piece_ref, offset) in enumerate(zip(pieces, offsets)):
        chunks = chunk_pair((band // 2 + offset + ZS) % ZS, band % 2, tile)
        for part in range(2):
            weights = piece_ref[part * 256 : (part + 1) * 256, :]
            both = jnp.concatenate([weights, weights], axis=1)
            half = jnp.dot(both, m_ref[...], preferred_element_type=jnp.float32) + half_b1
            hidden = (half + half * jnp.tanh(half)).astype(jnp.bfloat16)
            second = jnp.dot(hidden, w2_ref[...], preferred_element_type=jnp.float32)
            headed = lax.dot_general(
                hidden, head_ref[...], CONTRACT_LANES, preferred_element_type=jnp.float32
            )
            mean = headed[:, 32:33] + headed[:, 48:49]
            centred = second + b2c - mean
            variance = jnp.mean(centred * centred, axis=1, keepdims=True)
            scale = lax.rsqrt(variance + 1e-05)
            flipped = jnp.where(lane == 64, scale, headed).T
            fields = flipped[0:16] + flipped[16:32] + shift
            fields = fields * flipped[64:65] + b_out
            start = pl.multiple_of(chunks[part] * 256, 256)
            slot = 2 * index + part
            staged[slot, :, 0, :] = fields[0:12]
            copies.append(
                pltpu.make_async_copy(
                    staged.at[slot], out_hbm.at[:, :, pl.ds(start, 256)], sems.at[slot]
                )
            )
            copies[-1].start()
    for copy in copies:
        copy.wait()


def decode_first_kernel(offsets, *refs):
    count = len(offsets)
    blocks_ref, w1_ref, w2_ref, head_ref, small_ref, out_hbm, m_ref, staged, sems = refs[count:]
    block = blocks_ref[0]
    for k in range(1, 8):
        block = block + blocks_ref[k]
    m = 0.5 * jnp.dot(block, w1_ref[...], preferred_element_type=jnp.float32)
    high, low = split(m)
    m_ref[0:128, :] = high
    m_ref[128:256, :] = low
    decode_pieces(refs[:count], offsets, m_ref, w2_ref, head_ref, small_ref, out_hbm, staged, sems)


def decode_more_kernel(offsets, *refs):
    count = len(offsets)
    m_ref, w2_ref, head_ref, small_ref, _, out_hbm, staged, sems = refs[count:]
    decode_pieces(refs[:count], offsets, m_ref, w2_ref, head_ref, small_ref, out_hbm, staged, sems)


FIELDS = jax.ShapeDtypeStruct((12, 1, 4096), jnp.float32)


def decode_scratch(count):
    return [
        pltpu.VMEM((2 * count, 12, 1, 256), jnp.float32),
        pltpu.SemaphoreType.DMA((2 * count,)),
    ]


def decode_cost(count):
    return pl.CostEstimate(
        flops=2 * count * 512 * (256 + 512 + 128) * 512, bytes_accessed=1 << 20, transcendentals=0
    )


def decode_first(offsets, pieces, blocks, w1, w2, head, small):
    count = len(pieces)
    return pl.pallas_call(
        lambda *refs: decode_first_kernel(offsets, *refs),
        out_shape=[FIELDS, jax.ShapeDtypeStruct((256, 512), jnp.bfloat16)],
        in_specs=[VMEM] * (count + 5),
        out_specs=[HBM, VMEM],
        scratch_shapes=decode_scratch(count),
        compiler_params=PARAMS,
        cost_estimate=decode_cost(count),
        name="decode_first",
    )(*pieces, blocks, w1, w2, head, small)


def decode_more(offsets, pieces, m, w2, head, small, fields):
    count = len(pieces)
    return pl.pallas_call(
        lambda *refs: decode_more_kernel(offsets, *refs),
        out_shape=FIELDS,
        in_specs=[VMEM] * (count + 4) + [HBM],
        out_specs=HBM,
        scratch_shapes=decode_scratch(count),
        input_output_aliases={count + 4: 0},
        compiler_params=PARAMS,
        cost_estimate=decode_cost(count),
        name="decode_more",
    )(*pieces, m, w2, head, small, fields)


def body(
    latents, owners, block_rows, interp_weights, w_first, b_first, w_second, b_second, gain,
    w_out, b_out,
):
    weights = interp_weights[0]
    near = lax.ppermute(weights, ("band", "patch"), scatter_pairs(0))
    far = lax.ppermute(weights, ("band", "patch"), scatter_pairs(1))
    mine, other, vectors = gather_rows(
        owners, block_rows, latents, b_first, b_second, gain, w_out, b_out
    )
    near, far, other = lax.optimization_barrier((near, far, other))
    swapped = lax.ppermute(other, "patch", [(p, p ^ 1) for p in range(16)])
    own = join(near, far)
    w1, w2, head, small = prepare(w_first, w_second, vectors)
    up, down = [own], [own]
    for step in range(3):
        up.append(lax.ppermute(up[-1], "band", along_z(1)))
        down.append(lax.ppermute(down[-1], "band", along_z(-1)))
        if step == 0:
            up[1], swapped, w1, w2, head, small = lax.optimization_barrier(
                (up[1], swapped, w1, w2, head, small)
            )
            packed = pack(mine, swapped)
    blocks = lax.all_to_all(
        packed, "patch", 0, 0, tiled=True,
        axis_index_groups=[[2 * i + core for i in range(8)] for core in range(2)],
    )
    last = lax.ppermute(up[3], "band", along_z(1))
    pieces = [own, up[1], down[1], up[2], down[2], up[3], down[3]]
    fields, m = decode_first([0, -1, 1, -2, 2, -3, 3], pieces, blocks, w1, w2, head, small)
    fields = decode_more([-4], [last], m, w2, head, small, fields)
    return jnp.transpose(fields, (1, 0, 2))


def solution(mesh):
    return jax.shard_map(
        body,
        mesh=mesh,
        in_specs=(
            P("band", "patch", None),
            P(),
            P(),
            P("band", "patch", None),
            P("band", None, None),
            P("band", None),
            P("band", None, None),
            P("band", None),
            P("band", None),
            P("band", None, None),
            P("band", None),
        ),
        out_specs=P("band", None, "patch"),
        check_vma=False,
    )
```

```python
import jax
import jax.numpy as jnp
from jax import lax
from jax.experimental import pallas as pl
from jax.experimental.pallas import tpu as pltpu
from jax.sharding import PartitionSpec as P

ZS = 8
DY_CORE = {0: (2, 0), 1: (2, 1), 2: (1, 0), 3: (1, 1), 7: (3, 0), 6: (3, 1), 5: (0, 0), 4: (0, 1)}
DZ_OF = {pair: dz for dz, pair in DY_CORE.items()}


def joint(z, x_lo, x_hi, y, core):
    return (z * 2 + x_lo) * 16 + x_hi * 8 + y * 2 + core


def scatter_pairs():
    pairs = []
    for tile in range(16):
        z_t, core_t = tile // 2, tile % 2
        xh_t, y_t = tile // 8, (tile // 2) % 4
        for xh in range(2):
            for y in range(4):
                for core in range(2):
                    dz = DZ_OF[((y - y_t) % 4, core)]
                    side = (core_t + (xh != xh_t)) % 2
                    pairs.append(
                        (
                            joint(z_t, core_t, xh, y, core),
                            joint((z_t + dz) % ZS, side, xh_t, y_t, core_t),
                        )
                    )
    return pairs


def along_z(shift):
    return [(b, ((b // 2 + shift) % ZS) * 2 + b % 2) for b in range(16)]


def to_chip(dx, dy):
    return [
        (p, ((p // 8) ^ dx) * 8 + (((p // 2) % 4 + dy) % 4) * 2 + p % 2) for p in range(16)
    ]


VMEM = pl.BlockSpec(memory_space=pltpu.VMEM)
HBM = pl.BlockSpec(memory_space=pltpu.HBM)
WIDE = pltpu.CompilerParams(vmem_limit_bytes=56 * 1024 * 1024)
PARAMS = pltpu.CompilerParams(vmem_limit_bytes=8 * 1024 * 1024)
CONTRACT_LANES = (((1,), (1,)), ((), ()))


def start_loads(pairs, sems):
    loads = [
        pltpu.make_async_copy(source, target, sems.at[i])
        for i, (source, target) in enumerate(pairs)
    ]
    for load in loads:
        load.start()
    return loads


def split(value):
    high = value.astype(jnp.bfloat16)
    return high, (value - high.astype(jnp.float32)).astype(jnp.bfloat16)


def gather_kernel(
    owners_hbm, rows_hbm, latents_hbm, b1_hbm, b2_hbm, gain_hbm, w_out_hbm, b_out_hbm,
    mine_ref, other_ref, vectors_ref,
    owners, rows_ref, latents_ref, chosen_ref,
    b1_ref, b2_ref, gain_ref, w_out_ref, b_out_ref, sems,
):
    loads = start_loads(
        [
            (owners_hbm, owners),
            (rows_hbm, rows_ref),
            (latents_hbm.at[0], latents_ref),
            (b1_hbm, b1_ref),
            (b2_hbm, b2_ref),
            (gain_hbm, gain_ref),
            (w_out_hbm.at[0], w_out_ref),
            (b_out_hbm, b_out_ref),
        ],
        sems,
    )
    mine_ref[...] = jnp.zeros_like(mine_ref)
    other_ref[...] = jnp.zeros_like(other_ref)
    me = lax.axis_index("patch")
    row_id = lax.broadcasted_iota(jnp.int32, (128, 128), 0)
    col_id = lax.broadcasted_iota(jnp.int32, (128, 128), 1)
    lane = lax.broadcasted_iota(jnp.int32, (128, 2560), 1)
    loads[0].wait()
    loads[1].wait()

    def find(i, carry):
        count, tiles = carry
        mine = owners[i] == me
        tiles = tuple(jnp.where(mine & (count == s), i, tiles[s]) for s in range(4))
        return count + mine.astype(jnp.int32), tiles

    count, tiles = lax.fori_loop(0, 16, find, (jnp.int32(0), (jnp.int32(0),) * 4), unroll=True)
    for s in range(4):

        @pl.when(s < count)
        def _():
            rows = rows_ref[pl.ds(tiles[s], 1), :]
            column = jnp.sum(jnp.where(row_id == col_id, rows, 0), axis=1, keepdims=True)
            chosen_ref[s * 128 : (s + 1) * 128, :] = (
                (lane == column).astype(jnp.float32).astype(jnp.bfloat16)
            )

    loads[2].wait()
    for s in range(4):

        @pl.when(s < count)
        def _():
            block = jnp.dot(
                chosen_ref[s * 128 : (s + 1) * 128, :],
                latents_ref[...],
                preferred_element_type=jnp.float32,
            ).astype(jnp.bfloat16)
            chip = tiles[s] // 2
            here = tiles[s] % 2 == me % 2

            @pl.when(here)
            def _():
                mine_ref[chip] = block

            @pl.when(jnp.logical_not(here))
            def _():
                other_ref[chip] = block

    for load in loads[3:]:
        load.wait()
    row_id = lax.broadcasted_iota(jnp.int32, (16, 12), 0)
    col_id = lax.broadcasted_iota(jnp.int32, (16, 12), 1)
    b_out = jnp.sum(jnp.where(row_id == col_id, b_out_ref[...], 0.0), axis=1, keepdims=True)
    vectors_ref[0:8, :] = jnp.broadcast_to(0.5 * b1_ref[...], (8, 512))
    vectors_ref[8:16, :] = jnp.broadcast_to(b2_ref[...], (8, 512))
    vectors_ref[16:28, :] = gain_ref[...] * w_out_ref[...].astype(jnp.float32)
    vectors_ref[28:32, :] = jnp.zeros((4, 512), jnp.float32)
    vectors_ref[32:48, :] = jnp.broadcast_to(b_out, (16, 512))


VECTORS = ((48, 512), jnp.float32)


def gather_rows(owners, block_rows, latents, b1, b2, gain, w_out, b_out):
    blocks = jax.ShapeDtypeStruct((8, 128, 512), jnp.bfloat16)
    row = pltpu.VMEM((1, 512), jnp.float32)
    return pl.pallas_call(
        gather_kernel,
        out_shape=[blocks, blocks, jax.ShapeDtypeStruct(*VECTORS)],
        in_specs=[HBM] * 8,
        out_specs=[VMEM] * 3,
        scratch_shapes=[
            pltpu.SMEM((16,), jnp.int32),
            pltpu.VMEM((16, 128), jnp.int32),
            pltpu.VMEM((2560, 512), jnp.bfloat16),
            pltpu.VMEM((512, 2560), jnp.bfloat16),
            row,
            row,
            row,
            pltpu.VMEM((12, 512), jnp.bfloat16),
            pltpu.VMEM((1, 12), jnp.float32),
            pltpu.SemaphoreType.DMA((8,)),
        ],
        compiler_params=WIDE,
        name="gather_rows",
    )(owners, block_rows, latents, b1, b2, gain, w_out, b_out)


def prepare_kernel(w1_ref, w2_ref, vectors_ref, w1_out, w2_out, head_ref, small_ref):
    gw = vectors_ref[16:32, :]
    g1 = gw.astype(jnp.bfloat16)
    g2, g3 = split(gw - g1.astype(jnp.float32))
    ones = jnp.ones((16, 512), jnp.bfloat16)
    stacked = jnp.concatenate([g1, g2, g3, ones], axis=0)
    raw = lax.dot_general(stacked, w2_ref[0], CONTRACT_LANES, preferred_element_type=jnp.float32)
    w2_mean = raw[48:49] * (1.0 / 512)
    total = jnp.sum(gw, axis=1, keepdims=True)
    head = raw[0:16] + raw[16:32] + raw[32:48] - total * w2_mean
    high, low = split(head)
    mean_high, mean_low = split(jnp.broadcast_to(w2_mean, (16, 512)))
    pad = jnp.zeros((64, 512), jnp.bfloat16)
    head_ref[...] = jnp.concatenate([high, low, mean_high, mean_low, pad], axis=0)
    b2 = vectors_ref[8:9, :]
    b2c = b2 - jnp.mean(b2, axis=1, keepdims=True)
    shift = jnp.sum(gw * b2c, axis=1, keepdims=True)
    small_ref[0:8, :] = jnp.broadcast_to(b2c, (8, 512))
    small_ref[8:16, :] = vectors_ref[0:8, :]
    small_ref[16:32, :] = jnp.broadcast_to(shift, (16, 512))
    small_ref[32:48, :] = vectors_ref[32:48, :]
    w1_out[...] = w1_ref[0]
    w2_out[...] = w2_ref[0]


def prepare(w1, w2, vectors):
    square = jax.ShapeDtypeStruct((512, 512), jnp.bfloat16)
    return pl.pallas_call(
        prepare_kernel,
        out_shape=[
            square,
            square,
            jax.ShapeDtypeStruct((128, 512), jnp.bfloat16),
            jax.ShapeDtypeStruct(*VECTORS),
        ],
        in_specs=[VMEM] * 3,
        out_specs=[VMEM] * 4,
        compiler_params=PARAMS,
        cost_estimate=pl.CostEstimate(
            flops=2 * 64 * 512 * 512, bytes_accessed=4 * 1024 * 1024, transcendentals=0
        ),
        name="prepare",
    )(w1, w2, vectors)


def join_kernel(near_ref, far_ref, own_ref):
    own_ref[0:256, :] = near_ref[...]
    own_ref[256:512, :] = far_ref[...]


def join(near, far):
    return pl.pallas_call(
        join_kernel,
        out_shape=jax.ShapeDtypeStruct((512, 128), jnp.bfloat16),
        in_specs=[VMEM] * 2,
        out_specs=VMEM,
        compiler_params=PARAMS,
        name="join",
    )(near, far)


def pack_kernel(mine_ref, other_ref, blocks_ref):
    blocks_ref[...] = mine_ref[...] + other_ref[...]


def pack(mine, other):
    return pl.pallas_call(
        pack_kernel,
        out_shape=jax.ShapeDtypeStruct((8, 128, 512), jnp.bfloat16),
        in_specs=[VMEM] * 2,
        out_specs=VMEM,
        compiler_params=PARAMS,
        name="pack",
    )(mine, other)


def chunk_pair(z, x_lo, tile):
    z_t, core_t = tile // 2, tile % 2
    xh_t, y_t = tile // 8, (tile // 2) % 4
    dz = (z - z_t + ZS) % ZS
    dy = jnp.int32(0)
    core = jnp.int32(0)
    for key, (dy_k, core_k) in DY_CORE.items():
        dy = jnp.where(dz == key, dy_k, dy)
        core = jnp.where(dz == key, core_k, core)
    y = (y_t + dy) % 4
    near = xh_t * 8 + y * 2 + core
    far = (1 - xh_t) * 8 + y * 2 + core
    same = x_lo == core_t
    return jnp.where(same, near, far), jnp.where(same, far, near)


def decode_pieces(pieces, offsets, m_ref, w2_ref, head_ref, small_ref, out_hbm, staged, sems):
    band = lax.axis_index("band")
    tile = lax.axis_index("patch")
    lane = lax.broadcasted_iota(jnp.int32, (256, 128), 1)
    b2c = small_ref[0:1, :]
    half_b1 = small_ref[8:9, :]
    shift = small_ref[16:32, 0:1]
    b_out = small_ref[32:48, 0:1]
    copies = []
    for index, (piece_ref, offset) in enumerate(zip(pieces, offsets)):
        chunks = chunk_pair((band // 2 + offset + ZS) % ZS, band % 2, tile)
        for part in range(2):
            weights = piece_ref[part * 256 : (part + 1) * 256, :]
            both = jnp.concatenate([weights, weights], axis=1)
            half = jnp.dot(both, m_ref[...], preferred_element_type=jnp.float32) + half_b1
            hidden = (half + half * jnp.tanh(half)).astype(jnp.bfloat16)
            second = jnp.dot(hidden, w2_ref[...], preferred_element_type=jnp.float32)
            headed = lax.dot_general(
                hidden, head_ref[...], CONTRACT_LANES, preferred_element_type=jnp.float32
            )
            mean = headed[:, 32:33] + headed[:, 48:49]
            centred = second + b2c - mean
            variance = jnp.mean(centred * centred, axis=1, keepdims=True)
            scale = lax.rsqrt(variance + 1e-05)
            flipped = jnp.where(lane == 64, scale, headed).T
            fields = flipped[0:16] + flipped[16:32] + shift
            fields = fields * flipped[64:65] + b_out
            start = pl.multiple_of(chunks[part] * 256, 256)
            slot = 2 * index + part
            staged[slot, :, 0, :] = fields[0:12]
            copies.append(
                pltpu.make_async_copy(
                    staged.at[slot], out_hbm.at[:, :, pl.ds(start, 256)], sems.at[slot]
                )
            )
            copies[-1].start()
    for copy in copies:
        copy.wait()


def decode_first_kernel(offsets, *refs):
    count = len(offsets)
    blocks_ref, w1_ref, w2_ref, head_ref, small_ref, out_hbm, m_ref, staged, sems = refs[count:]
    block = blocks_ref[0]
    for k in range(1, 8):
        block = block + blocks_ref[k]
    m = 0.5 * jnp.dot(block, w1_ref[...], preferred_element_type=jnp.float32)
    high, low = split(m)
    m_ref[0:128, :] = high
    m_ref[128:256, :] = low
    decode_pieces(refs[:count], offsets, m_ref, w2_ref, head_ref, small_ref, out_hbm, staged, sems)


def decode_more_kernel(offsets, *refs):
    count = len(offsets)
    m_ref, w2_ref, head_ref, small_ref, _, out_hbm, staged, sems = refs[count:]
    decode_pieces(refs[:count], offsets, m_ref, w2_ref, head_ref, small_ref, out_hbm, staged, sems)


FIELDS = jax.ShapeDtypeStruct((12, 1, 4096), jnp.float32)


def decode_scratch(count):
    return [
        pltpu.VMEM((2 * count, 12, 1, 256), jnp.float32),
        pltpu.SemaphoreType.DMA((2 * count,)),
    ]


def decode_cost(count):
    return pl.CostEstimate(
        flops=2 * count * 512 * (256 + 512 + 128) * 512, bytes_accessed=1 << 20, transcendentals=0
    )


def decode_first(offsets, pieces, blocks, w1, w2, head, small):
    count = len(pieces)
    return pl.pallas_call(
        lambda *refs: decode_first_kernel(offsets, *refs),
        out_shape=[FIELDS, jax.ShapeDtypeStruct((256, 512), jnp.bfloat16)],
        in_specs=[VMEM] * (count + 5),
        out_specs=[HBM, VMEM],
        scratch_shapes=decode_scratch(count),
        compiler_params=PARAMS,
        cost_estimate=decode_cost(count),
        name="decode_first",
    )(*pieces, blocks, w1, w2, head, small)


def decode_more(offsets, pieces, m, w2, head, small, fields):
    count = len(pieces)
    return pl.pallas_call(
        lambda *refs: decode_more_kernel(offsets, *refs),
        out_shape=FIELDS,
        in_specs=[VMEM] * (count + 4) + [HBM],
        out_specs=HBM,
        scratch_shapes=decode_scratch(count),
        input_output_aliases={count + 4: 0},
        compiler_params=PARAMS,
        cost_estimate=decode_cost(count),
        name="decode_more",
    )(*pieces, m, w2, head, small, fields)


def body(
    latents, owners, block_rows, interp_weights, w_first, b_first, w_second, b_second, gain,
    w_out, b_out,
):
    weights = interp_weights[0]
    near = lax.ppermute(weights, ("band", "patch"), scatter_pairs())
    mine, other, vectors = gather_rows(
        owners, block_rows, latents, b_first, b_second, gain, w_out, b_out
    )
    near, other = lax.optimization_barrier((near, other))
    swapped = lax.ppermute(other, "patch", [(p, p ^ 1) for p in range(16)])
    far = lax.ppermute(near, "band", [(b, b ^ 1) for b in range(16)])
    w1, w2, head, small = prepare(w_first, w_second, vectors)
    swapped, near, far, w1, w2, head, small = lax.optimization_barrier(
        (swapped, near, far, w1, w2, head, small)
    )
    own = join(near, far)
    blocks = lax.all_to_all(
        pack(mine, swapped), "patch", 0, 0, tiled=True,
        axis_index_groups=[[2 * i + core for i in range(8)] for core in range(2)],
    )
    up, down = [own], [own]
    for step in range(3):
        up.append(lax.ppermute(up[-1], "band", along_z(1)))
        down.append(lax.ppermute(down[-1], "band", along_z(-1)))
    last = lax.ppermute(up[3], "band", along_z(1))
    pieces = [own, up[1], down[1], up[2], down[2], up[3], down[3]]
    fields, m = decode_first([0, -1, 1, -2, 2, -3, 3], pieces, blocks, w1, w2, head, small)
    fields = decode_more([-4], [last], m, w2, head, small, fields)
    return jnp.transpose(fields, (1, 0, 2))


def solution(mesh):
    return jax.shard_map(
        body,
        mesh=mesh,
        in_specs=(
            P("band", "patch", None),
            P(),
            P(),
            P("band", "patch", None),
            P("band", None, None),
            P("band", None),
            P("band", None, None),
            P("band", None),
            P("band", None),
            P("band", None, None),
            P("band", None),
        ),
        out_specs=P("band", None, "patch"),
        check_vma=False,
    )
```

```python
import jax
import jax.numpy as jnp
from jax import lax
from jax.experimental import pallas as pl
from jax.experimental.pallas import tpu as pltpu
from jax.sharding import PartitionSpec as P

ZS = 8
DY_CORE = {0: (2, 0), 1: (2, 1), 2: (1, 0), 3: (1, 1), 7: (3, 0), 6: (3, 1), 5: (0, 0), 4: (0, 1)}
DZ_OF = {pair: dz for dz, pair in DY_CORE.items()}


def joint(z, x_lo, x_hi, y, core):
    return (z * 2 + x_lo) * 16 + x_hi * 8 + y * 2 + core


def scatter_pairs():
    pairs = []
    for tile in range(16):
        z_t, core_t = tile // 2, tile % 2
        xh_t, y_t = tile // 8, (tile // 2) % 4
        for xh in range(2):
            for y in range(4):
                for core in range(2):
                    dz = DZ_OF[((y - y_t) % 4, core)]
                    side = (core_t + (xh != xh_t)) % 2
                    pairs.append(
                        (
                            joint(z_t, core_t, xh, y, core),
                            joint((z_t + dz) % ZS, side, xh_t, y_t, core_t),
                        )
                    )
    return pairs


def along_z(shift):
    return [(b, ((b // 2 + shift) % ZS) * 2 + b % 2) for b in range(16)]


def to_chip(dx, dy):
    return [
        (p, ((p // 8) ^ dx) * 8 + (((p // 2) % 4 + dy) % 4) * 2 + p % 2) for p in range(16)
    ]


VMEM = pl.BlockSpec(memory_space=pltpu.VMEM)
HBM = pl.BlockSpec(memory_space=pltpu.HBM)
WIDE = pltpu.CompilerParams(vmem_limit_bytes=56 * 1024 * 1024)
PARAMS = pltpu.CompilerParams(vmem_limit_bytes=8 * 1024 * 1024)
CONTRACT_LANES = (((1,), (1,)), ((), ()))


def start_loads(pairs, sems):
    loads = [
        pltpu.make_async_copy(source, target, sems.at[i])
        for i, (source, target) in enumerate(pairs)
    ]
    for load in loads:
        load.start()
    return loads


def split(value):
    high = value.astype(jnp.bfloat16)
    return high, (value - high.astype(jnp.float32)).astype(jnp.bfloat16)


def gather_kernel(
    owners_hbm, rows_hbm, latents_hbm, b1_hbm, b2_hbm, gain_hbm, w_out_hbm, b_out_hbm,
    mine_ref, other_ref, vectors_ref,
    owners, rows_ref, latents_ref, chosen_ref,
    b1_ref, b2_ref, gain_ref, w_out_ref, b_out_ref, sems,
):
    loads = start_loads(
        [
            (owners_hbm, owners),
            (rows_hbm, rows_ref),
            (latents_hbm.at[0], latents_ref),
            (b1_hbm, b1_ref),
            (b2_hbm, b2_ref),
            (gain_hbm, gain_ref),
            (w_out_hbm.at[0], w_out_ref),
            (b_out_hbm, b_out_ref),
        ],
        sems,
    )
    mine_ref[...] = jnp.zeros_like(mine_ref)
    other_ref[...] = jnp.zeros_like(other_ref)
    me = lax.axis_index("patch")
    row_id = lax.broadcasted_iota(jnp.int32, (128, 128), 0)
    col_id = lax.broadcasted_iota(jnp.int32, (128, 128), 1)
    lane = lax.broadcasted_iota(jnp.int32, (128, 2560), 1)
    loads[0].wait()
    loads[1].wait()

    def find(i, carry):
        count, tiles = carry
        mine = owners[i] == me
        tiles = tuple(jnp.where(mine & (count == s), i, tiles[s]) for s in range(4))
        return count + mine.astype(jnp.int32), tiles

    count, tiles = lax.fori_loop(0, 16, find, (jnp.int32(0), (jnp.int32(0),) * 4), unroll=True)
    for s in range(4):

        @pl.when(s < count)
        def _():
            rows = rows_ref[pl.ds(tiles[s], 1), :]
            column = jnp.sum(jnp.where(row_id == col_id, rows, 0), axis=1, keepdims=True)
            chosen_ref[s * 128 : (s + 1) * 128, :] = (
                (lane == column).astype(jnp.float32).astype(jnp.bfloat16)
            )

    loads[2].wait()
    for s in range(4):

        @pl.when(s < count)
        def _():
            block = jnp.dot(
                chosen_ref[s * 128 : (s + 1) * 128, :],
                latents_ref[...],
                preferred_element_type=jnp.float32,
            ).astype(jnp.bfloat16)
            chip = tiles[s] // 2
            here = tiles[s] % 2 == me % 2

            @pl.when(here)
            def _():
                mine_ref[chip] = block

            @pl.when(jnp.logical_not(here))
            def _():
                other_ref[chip] = block

    for load in loads[3:]:
        load.wait()
    row_id = lax.broadcasted_iota(jnp.int32, (16, 12), 0)
    col_id = lax.broadcasted_iota(jnp.int32, (16, 12), 1)
    b_out = jnp.sum(jnp.where(row_id == col_id, b_out_ref[...], 0.0), axis=1, keepdims=True)
    vectors_ref[0:8, :] = jnp.broadcast_to(0.5 * b1_ref[...], (8, 512))
    vectors_ref[8:16, :] = jnp.broadcast_to(b2_ref[...], (8, 512))
    vectors_ref[16:28, :] = gain_ref[...] * w_out_ref[...].astype(jnp.float32)
    vectors_ref[28:32, :] = jnp.zeros((4, 512), jnp.float32)
    vectors_ref[32:48, :] = jnp.broadcast_to(b_out, (16, 512))


VECTORS = ((48, 512), jnp.float32)


def gather_rows(owners, block_rows, latents, b1, b2, gain, w_out, b_out):
    blocks = jax.ShapeDtypeStruct((8, 128, 512), jnp.bfloat16)
    row = pltpu.VMEM((1, 512), jnp.float32)
    return pl.pallas_call(
        gather_kernel,
        out_shape=[blocks, blocks, jax.ShapeDtypeStruct(*VECTORS)],
        in_specs=[HBM] * 8,
        out_specs=[VMEM] * 3,
        scratch_shapes=[
            pltpu.SMEM((16,), jnp.int32),
            pltpu.VMEM((16, 128), jnp.int32),
            pltpu.VMEM((2560, 512), jnp.bfloat16),
            pltpu.VMEM((512, 2560), jnp.bfloat16),
            row,
            row,
            row,
            pltpu.VMEM((12, 512), jnp.bfloat16),
            pltpu.VMEM((1, 12), jnp.float32),
            pltpu.SemaphoreType.DMA((8,)),
        ],
        compiler_params=WIDE,
        name="gather_rows",
    )(owners, block_rows, latents, b1, b2, gain, w_out, b_out)


def prepare_kernel(w1_ref, w2_ref, vectors_ref, mine_ref, w1_out, w2_out, head_ref, small_ref, mine_out):
    gw = vectors_ref[16:32, :]
    g1 = gw.astype(jnp.bfloat16)
    g2, g3 = split(gw - g1.astype(jnp.float32))
    ones = jnp.ones((16, 512), jnp.bfloat16)
    stacked = jnp.concatenate([g1, g2, g3, ones], axis=0)
    raw = lax.dot_general(stacked, w2_ref[0], CONTRACT_LANES, preferred_element_type=jnp.float32)
    w2_mean = raw[48:49] * (1.0 / 512)
    total = jnp.sum(gw, axis=1, keepdims=True)
    head = raw[0:16] + raw[16:32] + raw[32:48] - total * w2_mean
    high, low = split(head)
    mean_high, mean_low = split(jnp.broadcast_to(w2_mean, (16, 512)))
    pad = jnp.zeros((64, 512), jnp.bfloat16)
    head_ref[...] = jnp.concatenate([high, low, mean_high, mean_low, pad], axis=0)
    b2 = vectors_ref[8:9, :]
    b2c = b2 - jnp.mean(b2, axis=1, keepdims=True)
    shift = jnp.sum(gw * b2c, axis=1, keepdims=True)
    small_ref[0:8, :] = jnp.broadcast_to(b2c, (8, 512))
    small_ref[8:16, :] = vectors_ref[0:8, :]
    small_ref[16:32, :] = jnp.broadcast_to(shift, (16, 512))
    small_ref[32:48, :] = vectors_ref[32:48, :]
    w1_out[...] = w1_ref[0]
    w2_out[...] = w2_ref[0]
    mine_out[...] = mine_ref[...]


def prepare(w1, w2, vectors, mine):
    square = jax.ShapeDtypeStruct((512, 512), jnp.bfloat16)
    return pl.pallas_call(
        prepare_kernel,
        out_shape=[
            square,
            square,
            jax.ShapeDtypeStruct((128, 512), jnp.bfloat16),
            jax.ShapeDtypeStruct(*VECTORS),
            jax.ShapeDtypeStruct((8, 128, 512), jnp.bfloat16),
        ],
        in_specs=[VMEM] * 4,
        out_specs=[VMEM] * 5,
        compiler_params=PARAMS,
        cost_estimate=pl.CostEstimate(
            flops=2 * 64 * 512 * 512, bytes_accessed=4 * 1024 * 1024, transcendentals=0
        ),
        name="prepare",
    )(w1, w2, vectors, mine)


def join_kernel(near_ref, far_ref, own_ref):
    own_ref[0:256, :] = near_ref[...]
    own_ref[256:512, :] = far_ref[...]


def join(near, far):
    return pl.pallas_call(
        join_kernel,
        out_shape=jax.ShapeDtypeStruct((512, 128), jnp.bfloat16),
        in_specs=[VMEM] * 2,
        out_specs=VMEM,
        compiler_params=PARAMS,
        name="join",
    )(near, far)


def pack_kernel(mine_ref, other_ref, blocks_ref):
    blocks_ref[...] = mine_ref[...] + other_ref[...]


def pack(mine, other):
    return pl.pallas_call(
        pack_kernel,
        out_shape=jax.ShapeDtypeStruct((8, 128, 512), jnp.bfloat16),
        in_specs=[VMEM] * 2,
        out_specs=VMEM,
        compiler_params=PARAMS,
        name="pack",
    )(mine, other)


def chunk_pair(z, x_lo, tile):
    z_t, core_t = tile // 2, tile % 2
    xh_t, y_t = tile // 8, (tile // 2) % 4
    dz = (z - z_t + ZS) % ZS
    dy = jnp.int32(0)
    core = jnp.int32(0)
    for key, (dy_k, core_k) in DY_CORE.items():
        dy = jnp.where(dz == key, dy_k, dy)
        core = jnp.where(dz == key, core_k, core)
    y = (y_t + dy) % 4
    near = xh_t * 8 + y * 2 + core
    far = (1 - xh_t) * 8 + y * 2 + core
    same = x_lo == core_t
    return jnp.where(same, near, far), jnp.where(same, far, near)


def decode_pieces(pieces, offsets, m_ref, w2_ref, head_ref, small_ref, out_hbm, staged, sems):
    band = lax.axis_index("band")
    tile = lax.axis_index("patch")
    lane = lax.broadcasted_iota(jnp.int32, (512, 128), 1)
    b2c = small_ref[0:1, :]
    half_b1 = small_ref[8:9, :]
    shift = small_ref[16:32, 0:1]
    b_out = small_ref[32:48, 0:1]
    copies = []
    for index, (piece_ref, offset) in enumerate(zip(pieces, offsets)):
        chunks = chunk_pair((band // 2 + offset + ZS) % ZS, band % 2, tile)
        weights = piece_ref[...]
        both = jnp.concatenate([weights, weights], axis=1)
        half = jnp.dot(both, m_ref[...], preferred_element_type=jnp.float32) + half_b1
        hidden = (half + half * jnp.tanh(half)).astype(jnp.bfloat16)
        second = jnp.dot(hidden, w2_ref[...], preferred_element_type=jnp.float32)
        headed = lax.dot_general(
            hidden, head_ref[...], CONTRACT_LANES, preferred_element_type=jnp.float32
        )
        mean = headed[:, 32:33] + headed[:, 48:49]
        centred = second + b2c - mean
        variance = jnp.mean(centred * centred, axis=1, keepdims=True)
        scale = lax.rsqrt(variance + 1e-05)
        flipped = jnp.where(lane == 64, scale, headed).T
        fields = flipped[0:16] + flipped[16:32] + shift
        fields = fields * flipped[64:65] + b_out
        for part in range(2):
            start = pl.multiple_of(chunks[part] * 256, 256)
            slot = 2 * index + part
            staged[slot, :, 0, :] = fields[0:12, part * 256 : (part + 1) * 256]
            copies.append(
                pltpu.make_async_copy(
                    staged.at[slot], out_hbm.at[:, :, pl.ds(start, 256)], sems.at[slot]
                )
            )
            copies[-1].start()
    for copy in copies:
        copy.wait()


def decode_first_kernel(offsets, *refs):
    count = len(offsets)
    blocks_ref, w1_ref, w2_ref, head_ref, small_ref, out_hbm, m_ref, staged, sems = refs[count:]
    block = blocks_ref[0]
    for k in range(1, 8):
        block = block + blocks_ref[k]
    m = 0.5 * jnp.dot(block, w1_ref[...], preferred_element_type=jnp.float32)
    high, low = split(m)
    m_ref[0:128, :] = high
    m_ref[128:256, :] = low
    decode_pieces(refs[:count], offsets, m_ref, w2_ref, head_ref, small_ref, out_hbm, staged, sems)


def decode_more_kernel(offsets, *refs):
    count = len(offsets)
    m_ref, w2_ref, head_ref, small_ref, _, out_hbm, staged, sems = refs[count:]
    decode_pieces(refs[:count], offsets, m_ref, w2_ref, head_ref, small_ref, out_hbm, staged, sems)


FIELDS = jax.ShapeDtypeStruct((12, 1, 4096), jnp.float32)


def decode_scratch(count):
    return [
        pltpu.VMEM((2 * count, 12, 1, 256), jnp.float32),
        pltpu.SemaphoreType.DMA((2 * count,)),
    ]


def decode_cost(count):
    return pl.CostEstimate(
        flops=2 * count * 512 * (256 + 512 + 128) * 512, bytes_accessed=1 << 20, transcendentals=0
    )


def decode_first(offsets, pieces, blocks, w1, w2, head, small):
    count = len(pieces)
    return pl.pallas_call(
        lambda *refs: decode_first_kernel(offsets, *refs),
        out_shape=[FIELDS, jax.ShapeDtypeStruct((256, 512), jnp.bfloat16)],
        in_specs=[VMEM] * (count + 5),
        out_specs=[HBM, VMEM],
        scratch_shapes=decode_scratch(count),
        compiler_params=PARAMS,
        cost_estimate=decode_cost(count),
        name="decode_first",
    )(*pieces, blocks, w1, w2, head, small)


def decode_more(offsets, pieces, m, w2, head, small, fields):
    count = len(pieces)
    return pl.pallas_call(
        lambda *refs: decode_more_kernel(offsets, *refs),
        out_shape=FIELDS,
        in_specs=[VMEM] * (count + 4) + [HBM],
        out_specs=HBM,
        scratch_shapes=decode_scratch(count),
        input_output_aliases={count + 4: 0},
        compiler_params=PARAMS,
        cost_estimate=decode_cost(count),
        name="decode_more",
    )(*pieces, m, w2, head, small, fields)


def body(
    latents, owners, block_rows, interp_weights, w_first, b_first, w_second, b_second, gain,
    w_out, b_out,
):
    weights = interp_weights[0]
    near = lax.ppermute(weights, ("band", "patch"), scatter_pairs())
    mine, other, vectors = gather_rows(
        owners, block_rows, latents, b_first, b_second, gain, w_out, b_out
    )
    near, other = lax.optimization_barrier((near, other))
    swapped = lax.ppermute(other, "patch", [(p, p ^ 1) for p in range(16)])
    far = lax.ppermute(near, "band", [(b, b ^ 1) for b in range(16)])
    w1, w2, head, small, mine = prepare(w_first, w_second, vectors, mine)
    swapped, near, far, mine, w1, w2, head, small = lax.optimization_barrier(
        (swapped, near, far, mine, w1, w2, head, small)
    )
    own = join(near, far)
    blocks = lax.all_to_all(
        pack(mine, swapped), "patch", 0, 0, tiled=True,
        axis_index_groups=[[2 * i + core for i in range(8)] for core in range(2)],
    )
    up, down = [own], [own]
    for step in range(3):
        up.append(lax.ppermute(up[-1], "band", along_z(1)))
        down.append(lax.ppermute(down[-1], "band", along_z(-1)))
    last = lax.ppermute(up[3], "band", along_z(1))
    pieces = [own, up[1], down[1], up[2], down[2], up[3], down[3]]
    fields, m = decode_first([0, -1, 1, -2, 2, -3, 3], pieces, blocks, w1, w2, head, small)
    fields = decode_more([-4], [last], m, w2, head, small, fields)
    return jnp.transpose(fields, (1, 0, 2))


def solution(mesh):
    return jax.shard_map(
        body,
        mesh=mesh,
        in_specs=(
            P("band", "patch", None),
            P(),
            P(),
            P("band", "patch", None),
            P("band", None, None),
            P("band", None),
            P("band", None, None),
            P("band", None),
            P("band", None),
            P("band", None, None),
            P("band", None),
        ),
        out_specs=P("band", None, "patch"),
        check_vma=False,
    )
```

```python
import jax
import jax.numpy as jnp
from jax import lax
from jax.experimental import pallas as pl
from jax.experimental.pallas import tpu as pltpu
from jax.sharding import PartitionSpec as P

ZS = 8
DY_CORE = {0: (2, 0), 1: (2, 1), 2: (1, 0), 3: (1, 1), 7: (3, 0), 6: (3, 1), 5: (0, 0), 4: (0, 1)}
DZ_OF = {pair: dz for dz, pair in DY_CORE.items()}


def joint(z, x_lo, x_hi, y, core):
    return (z * 2 + x_lo) * 16 + x_hi * 8 + y * 2 + core


def scatter_pairs():
    pairs = []
    for tile in range(16):
        z_t, core_t = tile // 2, tile % 2
        xh_t, y_t = tile // 8, (tile // 2) % 4
        for xh in range(2):
            for y in range(4):
                for core in range(2):
                    dz = DZ_OF[((y - y_t) % 4, core)]
                    side = (core_t + (xh != xh_t)) % 2
                    pairs.append(
                        (
                            joint(z_t, core_t, xh, y, core),
                            joint((z_t + dz) % ZS, side, xh_t, y_t, core_t),
                        )
                    )
    return pairs


def along_z(shift):
    return [(b, ((b // 2 + shift) % ZS) * 2 + b % 2) for b in range(16)]


def to_chip(dx, dy):
    return [
        (p, ((p // 8) ^ dx) * 8 + (((p // 2) % 4 + dy) % 4) * 2 + p % 2) for p in range(16)
    ]


VMEM = pl.BlockSpec(memory_space=pltpu.VMEM)
HBM = pl.BlockSpec(memory_space=pltpu.HBM)
WIDE = pltpu.CompilerParams(vmem_limit_bytes=56 * 1024 * 1024)
PARAMS = pltpu.CompilerParams(vmem_limit_bytes=8 * 1024 * 1024)
CONTRACT_LANES = (((1,), (1,)), ((), ()))


def start_loads(pairs, sems):
    loads = [
        pltpu.make_async_copy(source, target, sems.at[i])
        for i, (source, target) in enumerate(pairs)
    ]
    for load in loads:
        load.start()
    return loads


def split(value):
    high = value.astype(jnp.bfloat16)
    return high, (value - high.astype(jnp.float32)).astype(jnp.bfloat16)


def gather_kernel(
    owners_hbm, rows_hbm, latents_hbm, b1_hbm, b2_hbm, gain_hbm, w_out_hbm, b_out_hbm,
    mine_ref, other_ref, vectors_ref,
    owners, rows_ref, latents_ref, chosen_ref,
    b1_ref, b2_ref, gain_ref, w_out_ref, b_out_ref, sems,
):
    loads = start_loads(
        [
            (owners_hbm, owners),
            (rows_hbm, rows_ref),
            (latents_hbm.at[0], latents_ref),
            (b1_hbm, b1_ref),
            (b2_hbm, b2_ref),
            (gain_hbm, gain_ref),
            (w_out_hbm.at[0], w_out_ref),
            (b_out_hbm, b_out_ref),
        ],
        sems,
    )
    mine_ref[...] = jnp.zeros_like(mine_ref)
    other_ref[...] = jnp.zeros_like(other_ref)
    me = lax.axis_index("patch")
    row_id = lax.broadcasted_iota(jnp.int32, (128, 128), 0)
    col_id = lax.broadcasted_iota(jnp.int32, (128, 128), 1)
    lane = lax.broadcasted_iota(jnp.int32, (128, 2560), 1)
    loads[0].wait()
    loads[1].wait()

    def find(i, carry):
        count, tiles = carry
        mine = owners[i] == me
        tiles = tuple(jnp.where(mine & (count == s), i, tiles[s]) for s in range(4))
        return count + mine.astype(jnp.int32), tiles

    count, tiles = lax.fori_loop(0, 16, find, (jnp.int32(0), (jnp.int32(0),) * 4), unroll=True)
    for s in range(4):

        @pl.when(s < count)
        def _():
            rows = rows_ref[pl.ds(tiles[s], 1), :]
            column = jnp.sum(jnp.where(row_id == col_id, rows, 0), axis=1, keepdims=True)
            chosen_ref[s * 128 : (s + 1) * 128, :] = (
                (lane == column).astype(jnp.float32).astype(jnp.bfloat16)
            )

    loads[2].wait()
    for s in range(4):

        @pl.when(s < count)
        def _():
            block = jnp.dot(
                chosen_ref[s * 128 : (s + 1) * 128, :],
                latents_ref[...],
                preferred_element_type=jnp.float32,
            ).astype(jnp.bfloat16)
            chip = tiles[s] // 2
            here = tiles[s] % 2 == me % 2

            @pl.when(here)
            def _():
                mine_ref[chip] = block

            @pl.when(jnp.logical_not(here))
            def _():
                other_ref[chip] = block

    for load in loads[3:]:
        load.wait()
    row_id = lax.broadcasted_iota(jnp.int32, (16, 12), 0)
    col_id = lax.broadcasted_iota(jnp.int32, (16, 12), 1)
    b_out = jnp.sum(jnp.where(row_id == col_id, b_out_ref[...], 0.0), axis=1, keepdims=True)
    vectors_ref[0:8, :] = jnp.broadcast_to(0.5 * b1_ref[...], (8, 512))
    vectors_ref[8:16, :] = jnp.broadcast_to(b2_ref[...], (8, 512))
    vectors_ref[16:28, :] = gain_ref[...] * w_out_ref[...].astype(jnp.float32)
    vectors_ref[28:32, :] = jnp.zeros((4, 512), jnp.float32)
    vectors_ref[32:48, :] = jnp.broadcast_to(b_out, (16, 512))


VECTORS = ((48, 512), jnp.float32)


def gather_rows(owners, block_rows, latents, b1, b2, gain, w_out, b_out):
    blocks = jax.ShapeDtypeStruct((8, 128, 512), jnp.bfloat16)
    row = pltpu.VMEM((1, 512), jnp.float32)
    return pl.pallas_call(
        gather_kernel,
        out_shape=[blocks, blocks, jax.ShapeDtypeStruct(*VECTORS)],
        in_specs=[HBM] * 8,
        out_specs=[VMEM] * 3,
        scratch_shapes=[
            pltpu.SMEM((16,), jnp.int32),
            pltpu.VMEM((16, 128), jnp.int32),
            pltpu.VMEM((2560, 512), jnp.bfloat16),
            pltpu.VMEM((512, 2560), jnp.bfloat16),
            row,
            row,
            row,
            pltpu.VMEM((12, 512), jnp.bfloat16),
            pltpu.VMEM((1, 12), jnp.float32),
            pltpu.SemaphoreType.DMA((8,)),
        ],
        compiler_params=WIDE,
        name="gather_rows",
    )(owners, block_rows, latents, b1, b2, gain, w_out, b_out)


def prepare_kernel(w1_ref, w2_ref, vectors_ref, mine_ref, w1_out, w2_out, head_ref, small_ref, mine_out):
    gw = vectors_ref[16:32, :]
    g1 = gw.astype(jnp.bfloat16)
    g2, g3 = split(gw - g1.astype(jnp.float32))
    ones = jnp.ones((16, 512), jnp.bfloat16)
    stacked = jnp.concatenate([g1, g2, g3, ones], axis=0)
    raw = lax.dot_general(stacked, w2_ref[0], CONTRACT_LANES, preferred_element_type=jnp.float32)
    w2_mean = raw[48:49] * (1.0 / 512)
    total = jnp.sum(gw, axis=1, keepdims=True)
    head = raw[0:16] + raw[16:32] + raw[32:48] - total * w2_mean
    high, low = split(head)
    mean_high, mean_low = split(jnp.broadcast_to(w2_mean, (16, 512)))
    pad = jnp.zeros((64, 512), jnp.bfloat16)
    head_ref[...] = jnp.concatenate([high, low, mean_high, mean_low, pad], axis=0)
    b2 = vectors_ref[8:9, :]
    b2c = b2 - jnp.mean(b2, axis=1, keepdims=True)
    shift = jnp.sum(gw * b2c, axis=1, keepdims=True)
    small_ref[0:8, :] = jnp.broadcast_to(b2c, (8, 512))
    small_ref[8:16, :] = vectors_ref[0:8, :]
    small_ref[16:32, :] = jnp.broadcast_to(shift, (16, 512))
    small_ref[32:48, :] = vectors_ref[32:48, :]
    w1_out[...] = w1_ref[0]
    w2_out[...] = w2_ref[0]
    mine_out[...] = mine_ref[...]


def prepare(w1, w2, vectors, mine):
    square = jax.ShapeDtypeStruct((512, 512), jnp.bfloat16)
    return pl.pallas_call(
        prepare_kernel,
        out_shape=[
            square,
            square,
            jax.ShapeDtypeStruct((128, 512), jnp.bfloat16),
            jax.ShapeDtypeStruct(*VECTORS),
            jax.ShapeDtypeStruct((8, 128, 512), jnp.bfloat16),
        ],
        in_specs=[VMEM] * 4,
        out_specs=[VMEM] * 5,
        compiler_params=PARAMS,
        cost_estimate=pl.CostEstimate(
            flops=2 * 64 * 512 * 512, bytes_accessed=4 * 1024 * 1024, transcendentals=0
        ),
        name="prepare",
    )(w1, w2, vectors, mine)


def join_kernel(near_ref, far_ref, own_ref):
    own_ref[0:256, :] = near_ref[...]
    own_ref[256:512, :] = far_ref[...]


def join(near, far):
    return pl.pallas_call(
        join_kernel,
        out_shape=jax.ShapeDtypeStruct((512, 128), jnp.bfloat16),
        in_specs=[VMEM] * 2,
        out_specs=VMEM,
        compiler_params=PARAMS,
        name="join",
    )(near, far)


def pack_kernel(mine_ref, other_ref, blocks_ref):
    blocks_ref[...] = mine_ref[...] + other_ref[...]


def pack(mine, other):
    return pl.pallas_call(
        pack_kernel,
        out_shape=jax.ShapeDtypeStruct((8, 128, 512), jnp.bfloat16),
        in_specs=[VMEM] * 2,
        out_specs=VMEM,
        compiler_params=PARAMS,
        name="pack",
    )(mine, other)


def chunk_pair(z, x_lo, tile):
    z_t, core_t = tile // 2, tile % 2
    xh_t, y_t = tile // 8, (tile // 2) % 4
    dz = (z - z_t + ZS) % ZS
    dy = jnp.int32(0)
    core = jnp.int32(0)
    for key, (dy_k, core_k) in DY_CORE.items():
        dy = jnp.where(dz == key, dy_k, dy)
        core = jnp.where(dz == key, core_k, core)
    y = (y_t + dy) % 4
    near = xh_t * 8 + y * 2 + core
    far = (1 - xh_t) * 8 + y * 2 + core
    same = x_lo == core_t
    return jnp.where(same, near, far), jnp.where(same, far, near)


def decode_pieces(pieces, offsets, m_ref, w2_ref, head_ref, small_ref, staged, done):
    band = lax.axis_index("band")
    tile = lax.axis_index("patch")
    lane = lax.broadcasted_iota(jnp.int32, (512, 128), 1)
    b2c = small_ref[0:1, :]
    half_b1 = small_ref[8:9, :]
    shift = small_ref[16:32, 0:1]
    b_out = small_ref[32:48, 0:1]
    for index, (piece_ref, offset) in enumerate(zip(pieces, offsets)):
        chunks = chunk_pair((band // 2 + offset + ZS) % ZS, band % 2, tile)
        weights = piece_ref[...]
        both = jnp.concatenate([weights, weights], axis=1)
        half = jnp.dot(both, m_ref[...], preferred_element_type=jnp.float32) + half_b1
        hidden = (half + half * jnp.tanh(half)).astype(jnp.bfloat16)
        second = jnp.dot(hidden, w2_ref[...], preferred_element_type=jnp.float32)
        headed = lax.dot_general(
            hidden, head_ref[...], CONTRACT_LANES, preferred_element_type=jnp.float32
        )
        mean = headed[:, 32:33] + headed[:, 48:49]
        centred = second + b2c - mean
        variance = jnp.mean(centred * centred, axis=1, keepdims=True)
        scale = lax.rsqrt(variance + 1e-05)
        flipped = jnp.where(lane == 64, scale, headed).T
        fields = flipped[0:16] + flipped[16:32] + shift
        fields = fields * flipped[64:65] + b_out
        for part in range(2):
            start = pl.multiple_of(chunks[part] * 256, 256)
            slot = 2 * index + part
            staged[slot, :, 0, :] = fields[0:12, part * 256 : (part + 1) * 256]
            done(slot, start)


def first_layer_kernel(blocks_ref, w1_ref, m_ref):
    block = blocks_ref[0]
    for k in range(1, 8):
        block = block + blocks_ref[k]
    m = 0.5 * jnp.dot(block, w1_ref[...], preferred_element_type=jnp.float32)
    high, low = split(m)
    m_ref[0:128, :] = high
    m_ref[128:256, :] = low


def first_layer(blocks, w1):
    return pl.pallas_call(
        first_layer_kernel,
        out_shape=jax.ShapeDtypeStruct((256, 512), jnp.bfloat16),
        in_specs=[VMEM] * 2,
        out_specs=VMEM,
        compiler_params=PARAMS,
        name="first_layer",
    )(blocks, w1)


def decode_first_kernel(offsets, *refs):
    count = len(offsets)
    m_ref, w2_ref, head_ref, small_ref, staged = refs[count:]
    decode_pieces(
        refs[:count], offsets, m_ref, w2_ref, head_ref, small_ref, staged, lambda slot, start: None
    )


def decode_last_kernel(earlier, offsets, *refs):
    count = len(offsets)
    m_ref, w2_ref, head_ref, small_ref, before, out_hbm, staged, sems = refs[count:]
    band = lax.axis_index("band")
    tile = lax.axis_index("patch")
    copies = []

    def send(source, start):
        copies.append(
            pltpu.make_async_copy(
                source, out_hbm.at[:, :, pl.ds(start, 256)], sems.at[len(copies)]
            )
        )
        copies[-1].start()

    for index, offset in enumerate(earlier):
        chunks = chunk_pair((band // 2 + offset + ZS) % ZS, band % 2, tile)
        for part in range(2):
            send(before.at[2 * index + part], pl.multiple_of(chunks[part] * 256, 256))
    decode_pieces(
        refs[:count], offsets, m_ref, w2_ref, head_ref, small_ref, staged,
        lambda slot, start: send(staged.at[slot], start),
    )
    for copy in copies:
        copy.wait()


FIELDS = jax.ShapeDtypeStruct((12, 1, 4096), jnp.float32)


def decode_cost(count):
    return pl.CostEstimate(
        flops=2 * count * 512 * (256 + 512 + 128) * 512, bytes_accessed=1 << 20, transcendentals=0
    )


def decode_first(offsets, pieces, m, w2, head, small):
    count = len(pieces)
    return pl.pallas_call(
        lambda *refs: decode_first_kernel(offsets, *refs),
        out_shape=jax.ShapeDtypeStruct((2 * count, 12, 1, 256), jnp.float32),
        in_specs=[VMEM] * (count + 4),
        out_specs=VMEM,
        compiler_params=PARAMS,
        cost_estimate=decode_cost(count),
        name="decode_first",
    )(*pieces, m, w2, head, small)


def decode_last(earlier, offsets, pieces, m, w2, head, small, before):
    count = len(pieces)
    return pl.pallas_call(
        lambda *refs: decode_last_kernel(earlier, offsets, *refs),
        out_shape=FIELDS,
        in_specs=[VMEM] * (count + 5),
        out_specs=HBM,
        scratch_shapes=[
            pltpu.VMEM((2 * count, 12, 1, 256), jnp.float32),
            pltpu.SemaphoreType.DMA((2 * (count + len(earlier)),)),
        ],
        compiler_params=PARAMS,
        cost_estimate=decode_cost(count),
        name="decode_last",
    )(*pieces, m, w2, head, small, before)


def body(
    latents, owners, block_rows, interp_weights, w_first, b_first, w_second, b_second, gain,
    w_out, b_out,
):
    weights = interp_weights[0]
    near = lax.ppermute(weights, ("band", "patch"), scatter_pairs())
    mine, other, vectors = gather_rows(
        owners, block_rows, latents, b_first, b_second, gain, w_out, b_out
    )
    near, other = lax.optimization_barrier((near, other))
    swapped = lax.ppermute(other, "patch", [(p, p ^ 1) for p in range(16)])
    far = lax.ppermute(near, "band", [(b, b ^ 1) for b in range(16)])
    w1, w2, head, small, mine = prepare(w_first, w_second, vectors, mine)
    swapped, near, far, mine, w1, w2, head, small = lax.optimization_barrier(
        (swapped, near, far, mine, w1, w2, head, small)
    )
    own = join(near, far)
    blocks = lax.all_to_all(
        pack(mine, swapped), "patch", 0, 0, tiled=True,
        axis_index_groups=[[2 * i + core for i in range(8)] for core in range(2)],
    )
    up, down = [own], [own]
    for step in range(3):
        up.append(lax.ppermute(up[-1], "band", along_z(1)))
        down.append(lax.ppermute(down[-1], "band", along_z(-1)))
    m = first_layer(blocks, w1)
    up[3], m = lax.optimization_barrier((up[3], m))
    last = lax.ppermute(up[3], "band", along_z(1))
    pieces = [own, up[1], down[1], up[2], down[2], up[3], down[3]]
    earlier = [0, -1, 1, -2, 2, -3, 3]
    before = decode_first(earlier, pieces, m, w2, head, small)
    fields = decode_last(earlier, [-4], [last], m, w2, head, small, before)
    return jnp.transpose(fields, (1, 0, 2))


def solution(mesh):
    return jax.shard_map(
        body,
        mesh=mesh,
        in_specs=(
            P("band", "patch", None),
            P(),
            P(),
            P("band", "patch", None),
            P("band", None, None),
            P("band", None),
            P("band", None, None),
            P("band", None),
            P("band", None),
            P("band", None, None),
            P("band", None),
        ),
        out_specs=P("band", None, "patch"),
        check_vma=False,
    )
```

```python
import jax
import jax.numpy as jnp
from jax import lax
from jax.experimental import pallas as pl
from jax.experimental.pallas import tpu as pltpu
from jax.sharding import PartitionSpec as P

ZS = 8
DY_CORE = {0: (2, 0), 1: (2, 1), 2: (1, 0), 3: (1, 1), 7: (3, 0), 6: (3, 1), 5: (0, 0), 4: (0, 1)}
DZ_OF = {pair: dz for dz, pair in DY_CORE.items()}


def joint(z, x_lo, x_hi, y, core):
    return (z * 2 + x_lo) * 16 + x_hi * 8 + y * 2 + core


def scatter_pairs():
    pairs = []
    for tile in range(16):
        z_t, core_t = tile // 2, tile % 2
        xh_t, y_t = tile // 8, (tile // 2) % 4
        for xh in range(2):
            for y in range(4):
                for core in range(2):
                    dz = DZ_OF[((y - y_t) % 4, core)]
                    side = (core_t + (xh != xh_t)) % 2
                    pairs.append(
                        (
                            joint(z_t, core_t, xh, y, core),
                            joint((z_t + dz) % ZS, side, xh_t, y_t, core_t),
                        )
                    )
    return pairs


def along_z(shift):
    return [(b, ((b // 2 + shift) % ZS) * 2 + b % 2) for b in range(16)]


def to_chip(dx, dy):
    return [
        (p, ((p // 8) ^ dx) * 8 + (((p // 2) % 4 + dy) % 4) * 2 + p % 2) for p in range(16)
    ]


VMEM = pl.BlockSpec(memory_space=pltpu.VMEM)
HBM = pl.BlockSpec(memory_space=pltpu.HBM)
WIDE = pltpu.CompilerParams(vmem_limit_bytes=56 * 1024 * 1024)
PARAMS = pltpu.CompilerParams(vmem_limit_bytes=8 * 1024 * 1024)
CONTRACT_LANES = (((1,), (1,)), ((), ()))


def start_loads(pairs, sems):
    loads = [
        pltpu.make_async_copy(source, target, sems.at[i])
        for i, (source, target) in enumerate(pairs)
    ]
    for load in loads:
        load.start()
    return loads


def split(value):
    high = value.astype(jnp.bfloat16)
    return high, (value - high.astype(jnp.float32)).astype(jnp.bfloat16)


def gather_kernel(
    owners_hbm, rows_hbm, latents_hbm, b1_hbm, b2_hbm, gain_hbm, w_out_hbm, b_out_hbm,
    mine_ref, other_ref, vectors_ref,
    owners, rows_ref, latents_ref, chosen_ref,
    b1_ref, b2_ref, gain_ref, w_out_ref, b_out_ref, sems,
):
    loads = start_loads(
        [
            (owners_hbm, owners),
            (rows_hbm, rows_ref),
            (latents_hbm.at[0], latents_ref),
            (b1_hbm, b1_ref),
            (b2_hbm, b2_ref),
            (gain_hbm, gain_ref),
            (w_out_hbm.at[0], w_out_ref),
            (b_out_hbm, b_out_ref),
        ],
        sems,
    )
    mine_ref[...] = jnp.zeros_like(mine_ref)
    other_ref[...] = jnp.zeros_like(other_ref)
    me = lax.axis_index("patch")
    row_id = lax.broadcasted_iota(jnp.int32, (128, 128), 0)
    col_id = lax.broadcasted_iota(jnp.int32, (128, 128), 1)
    lane = lax.broadcasted_iota(jnp.int32, (128, 2560), 1)
    loads[0].wait()
    loads[1].wait()

    def find(i, carry):
        count, tiles = carry
        mine = owners[i] == me
        tiles = tuple(jnp.where(mine & (count == s), i, tiles[s]) for s in range(4))
        return count + mine.astype(jnp.int32), tiles

    count, tiles = lax.fori_loop(0, 16, find, (jnp.int32(0), (jnp.int32(0),) * 4), unroll=True)
    for s in range(4):

        @pl.when(s < count)
        def _():
            rows = rows_ref[pl.ds(tiles[s], 1), :]
            column = jnp.sum(jnp.where(row_id == col_id, rows, 0), axis=1, keepdims=True)
            chosen_ref[s * 128 : (s + 1) * 128, :] = (
                (lane == column).astype(jnp.float32).astype(jnp.bfloat16)
            )

    loads[2].wait()
    for s in range(4):

        @pl.when(s < count)
        def _():
            block = jnp.dot(
                chosen_ref[s * 128 : (s + 1) * 128, :],
                latents_ref[...],
                preferred_element_type=jnp.float32,
            ).astype(jnp.bfloat16)
            chip = tiles[s] // 2
            here = tiles[s] % 2 == me % 2

            @pl.when(here)
            def _():
                mine_ref[chip] = block

            @pl.when(jnp.logical_not(here))
            def _():
                other_ref[chip] = block

    for load in loads[3:]:
        load.wait()
    row_id = lax.broadcasted_iota(jnp.int32, (16, 12), 0)
    col_id = lax.broadcasted_iota(jnp.int32, (16, 12), 1)
    b_out = jnp.sum(jnp.where(row_id == col_id, b_out_ref[...], 0.0), axis=1, keepdims=True)
    vectors_ref[0:8, :] = jnp.broadcast_to(0.5 * b1_ref[...], (8, 512))
    vectors_ref[8:16, :] = jnp.broadcast_to(b2_ref[...], (8, 512))
    vectors_ref[16:28, :] = gain_ref[...] * w_out_ref[...].astype(jnp.float32)
    vectors_ref[28:32, :] = jnp.zeros((4, 512), jnp.float32)
    vectors_ref[32:48, :] = jnp.broadcast_to(b_out, (16, 512))


VECTORS = ((48, 512), jnp.float32)


def gather_rows(owners, block_rows, latents, b1, b2, gain, w_out, b_out):
    blocks = jax.ShapeDtypeStruct((8, 128, 512), jnp.bfloat16)
    row = pltpu.VMEM((1, 512), jnp.float32)
    return pl.pallas_call(
        gather_kernel,
        out_shape=[blocks, blocks, jax.ShapeDtypeStruct(*VECTORS)],
        in_specs=[HBM] * 8,
        out_specs=[VMEM] * 3,
        scratch_shapes=[
            pltpu.SMEM((16,), jnp.int32),
            pltpu.VMEM((16, 128), jnp.int32),
            pltpu.VMEM((2560, 512), jnp.bfloat16),
            pltpu.VMEM((512, 2560), jnp.bfloat16),
            row,
            row,
            row,
            pltpu.VMEM((12, 512), jnp.bfloat16),
            pltpu.VMEM((1, 12), jnp.float32),
            pltpu.SemaphoreType.DMA((8,)),
        ],
        compiler_params=WIDE,
        name="gather_rows",
    )(owners, block_rows, latents, b1, b2, gain, w_out, b_out)


def prepare_kernel(w1_ref, w2_ref, vectors_ref, mine_ref, w1_out, w2_out, head_ref, small_ref, mine_out):
    gw = vectors_ref[16:32, :]
    g1 = gw.astype(jnp.bfloat16)
    g2, g3 = split(gw - g1.astype(jnp.float32))
    ones = jnp.ones((16, 512), jnp.bfloat16)
    stacked = jnp.concatenate([g1, g2, g3, ones], axis=0)
    raw = lax.dot_general(stacked, w2_ref[0], CONTRACT_LANES, preferred_element_type=jnp.float32)
    w2_mean = raw[48:49] * (1.0 / 512)
    total = jnp.sum(gw, axis=1, keepdims=True)
    head = raw[0:16] + raw[16:32] + raw[32:48] - total * w2_mean
    high, low = split(head)
    mean_high, mean_low = split(jnp.broadcast_to(w2_mean, (16, 512)))
    pad = jnp.zeros((64, 512), jnp.bfloat16)
    head_ref[...] = jnp.concatenate([high, low, mean_high, mean_low, pad], axis=0)
    b2 = vectors_ref[8:9, :]
    b2c = b2 - jnp.mean(b2, axis=1, keepdims=True)
    shift = jnp.sum(gw * b2c, axis=1, keepdims=True)
    small_ref[0:8, :] = jnp.broadcast_to(b2c, (8, 512))
    small_ref[8:16, :] = vectors_ref[0:8, :]
    small_ref[16:32, :] = jnp.broadcast_to(shift, (16, 512))
    small_ref[32:48, :] = vectors_ref[32:48, :]
    w1_out[...] = w1_ref[0]
    w2_out[...] = w2_ref[0]
    mine_out[...] = mine_ref[...]


def prepare(w1, w2, vectors, mine):
    square = jax.ShapeDtypeStruct((512, 512), jnp.bfloat16)
    return pl.pallas_call(
        prepare_kernel,
        out_shape=[
            square,
            square,
            jax.ShapeDtypeStruct((128, 512), jnp.bfloat16),
            jax.ShapeDtypeStruct(*VECTORS),
            jax.ShapeDtypeStruct((8, 128, 512), jnp.bfloat16),
        ],
        in_specs=[VMEM] * 4,
        out_specs=[VMEM] * 5,
        compiler_params=PARAMS,
        cost_estimate=pl.CostEstimate(
            flops=2 * 64 * 512 * 512, bytes_accessed=4 * 1024 * 1024, transcendentals=0
        ),
        name="prepare",
    )(w1, w2, vectors, mine)


def join_kernel(near_ref, far_ref, own_ref):
    own_ref[0:256, :] = near_ref[...]
    own_ref[256:512, :] = far_ref[...]


def join(near, far):
    return pl.pallas_call(
        join_kernel,
        out_shape=jax.ShapeDtypeStruct((512, 128), jnp.bfloat16),
        in_specs=[VMEM] * 2,
        out_specs=VMEM,
        compiler_params=PARAMS,
        name="join",
    )(near, far)


def pack_kernel(mine_ref, other_ref, blocks_hbm, blocks_ref, sems):
    copies = []
    for i in range(4):
        part = pl.ds(2 * i, 2)
        blocks_ref[part] = mine_ref[part] + other_ref[part]
        copies.append(
            pltpu.make_async_copy(blocks_ref.at[part], blocks_hbm.at[part], sems.at[i])
        )
        copies[-1].start()
    for copy in copies:
        copy.wait()


def pack(mine, other):
    shape = ((8, 128, 512), jnp.bfloat16)
    return pl.pallas_call(
        pack_kernel,
        out_shape=jax.ShapeDtypeStruct(*shape),
        in_specs=[VMEM] * 2,
        out_specs=HBM,
        scratch_shapes=[pltpu.VMEM(*shape), pltpu.SemaphoreType.DMA((4,))],
        compiler_params=PARAMS,
        name="pack",
    )(mine, other)


def chunk_pair(z, x_lo, tile):
    z_t, core_t = tile // 2, tile % 2
    xh_t, y_t = tile // 8, (tile // 2) % 4
    dz = (z - z_t + ZS) % ZS
    dy = jnp.int32(0)
    core = jnp.int32(0)
    for key, (dy_k, core_k) in DY_CORE.items():
        dy = jnp.where(dz == key, dy_k, dy)
        core = jnp.where(dz == key, core_k, core)
    y = (y_t + dy) % 4
    near = xh_t * 8 + y * 2 + core
    far = (1 - xh_t) * 8 + y * 2 + core
    same = x_lo == core_t
    return jnp.where(same, near, far), jnp.where(same, far, near)


def decode_pieces(pieces, offsets, m_ref, w2_ref, head_ref, small_ref, staged, done):
    band = lax.axis_index("band")
    tile = lax.axis_index("patch")
    lane = lax.broadcasted_iota(jnp.int32, (512, 128), 1)
    b2c = small_ref[0:1, :]
    half_b1 = small_ref[8:9, :]
    shift = small_ref[16:32, 0:1]
    b_out = small_ref[32:48, 0:1]
    for index, (piece_ref, offset) in enumerate(zip(pieces, offsets)):
        chunks = chunk_pair((band // 2 + offset + ZS) % ZS, band % 2, tile)
        weights = piece_ref[...]
        both = jnp.concatenate([weights, weights], axis=1)
        half = jnp.dot(both, m_ref[...], preferred_element_type=jnp.float32) + half_b1
        hidden = (half + half * jnp.tanh(half)).astype(jnp.bfloat16)
        second = jnp.dot(hidden, w2_ref[...], preferred_element_type=jnp.float32)
        headed = lax.dot_general(
            hidden, head_ref[...], CONTRACT_LANES, preferred_element_type=jnp.float32
        )
        mean = headed[:, 32:33] + headed[:, 48:49]
        centred = second + b2c - mean
        variance = jnp.mean(centred * centred, axis=1, keepdims=True)
        scale = lax.rsqrt(variance + 1e-05)
        flipped = jnp.where(lane == 64, scale, headed).T
        fields = flipped[0:16] + flipped[16:32] + shift
        fields = fields * flipped[64:65] + b_out
        for part in range(2):
            start = pl.multiple_of(chunks[part] * 256, 256)
            slot = 2 * index + part
            staged[slot, :, 0, :] = fields[0:12, part * 256 : (part + 1) * 256]
            done(slot, start)


def first_layer_kernel(blocks_ref, w1_ref, m_ref):
    block = blocks_ref[0]
    for k in range(1, 8):
        block = block + blocks_ref[k]
    m = 0.5 * jnp.dot(block, w1_ref[...], preferred_element_type=jnp.float32)
    high, low = split(m)
    m_ref[0:128, :] = high
    m_ref[128:256, :] = low


def first_layer(blocks, w1):
    return pl.pallas_call(
        first_layer_kernel,
        out_shape=jax.ShapeDtypeStruct((256, 512), jnp.bfloat16),
        in_specs=[VMEM] * 2,
        out_specs=VMEM,
        compiler_params=PARAMS,
        name="first_layer",
    )(blocks, w1)


def decode_first_kernel(offsets, *refs):
    count = len(offsets)
    m_ref, w2_ref, head_ref, small_ref, staged = refs[count:]
    decode_pieces(
        refs[:count], offsets, m_ref, w2_ref, head_ref, small_ref, staged, lambda slot, start: None
    )


def decode_last_kernel(earlier, offsets, *refs):
    count = len(offsets)
    m_ref, w2_ref, head_ref, small_ref, before, out_hbm, staged, sems = refs[count:]
    band = lax.axis_index("band")
    tile = lax.axis_index("patch")
    copies = []

    def send(source, start):
        copies.append(
            pltpu.make_async_copy(
                source, out_hbm.at[:, :, pl.ds(start, 256)], sems.at[len(copies)]
            )
        )
        copies[-1].start()

    for index, offset in enumerate(earlier):
        chunks = chunk_pair((band // 2 + offset + ZS) % ZS, band % 2, tile)
        for part in range(2):
            send(before.at[2 * index + part], pl.multiple_of(chunks[part] * 256, 256))
    decode_pieces(
        refs[:count], offsets, m_ref, w2_ref, head_ref, small_ref, staged,
        lambda slot, start: send(staged.at[slot], start),
    )
    for copy in copies:
        copy.wait()


FIELDS = jax.ShapeDtypeStruct((12, 1, 4096), jnp.float32)


def decode_cost(count):
    return pl.CostEstimate(
        flops=2 * count * 512 * (256 + 512 + 128) * 512, bytes_accessed=1 << 20, transcendentals=0
    )


def decode_first(offsets, pieces, m, w2, head, small):
    count = len(pieces)
    return pl.pallas_call(
        lambda *refs: decode_first_kernel(offsets, *refs),
        out_shape=jax.ShapeDtypeStruct((2 * count, 12, 1, 256), jnp.float32),
        in_specs=[VMEM] * (count + 4),
        out_specs=VMEM,
        compiler_params=PARAMS,
        cost_estimate=decode_cost(count),
        name="decode_first",
    )(*pieces, m, w2, head, small)


def decode_last(earlier, offsets, pieces, m, w2, head, small, before):
    count = len(pieces)
    return pl.pallas_call(
        lambda *refs: decode_last_kernel(earlier, offsets, *refs),
        out_shape=FIELDS,
        in_specs=[VMEM] * (count + 5),
        out_specs=HBM,
        scratch_shapes=[
            pltpu.VMEM((2 * count, 12, 1, 256), jnp.float32),
            pltpu.SemaphoreType.DMA((2 * (count + len(earlier)),)),
        ],
        compiler_params=PARAMS,
        cost_estimate=decode_cost(count),
        name="decode_last",
    )(*pieces, m, w2, head, small, before)


def body(
    latents, owners, block_rows, interp_weights, w_first, b_first, w_second, b_second, gain,
    w_out, b_out,
):
    weights = interp_weights[0]
    near = lax.ppermute(weights, ("band", "patch"), scatter_pairs())
    mine, other, vectors = gather_rows(
        owners, block_rows, latents, b_first, b_second, gain, w_out, b_out
    )
    near, other = lax.optimization_barrier((near, other))
    swapped = lax.ppermute(other, "patch", [(p, p ^ 1) for p in range(16)])
    far = lax.ppermute(near, "band", [(b, b ^ 1) for b in range(16)])
    w1, w2, head, small, mine = prepare(w_first, w_second, vectors, mine)
    swapped, near, far, mine, w1, w2, head, small = lax.optimization_barrier(
        (swapped, near, far, mine, w1, w2, head, small)
    )
    own = join(near, far)
    blocks = lax.all_to_all(
        pack(mine, swapped), "patch", 0, 0, tiled=True,
        axis_index_groups=[[2 * i + core for i in range(8)] for core in range(2)],
    )
    up, down = [own], [own]
    for step in range(3):
        up.append(lax.ppermute(up[-1], "band", along_z(1)))
        down.append(lax.ppermute(down[-1], "band", along_z(-1)))
    m = first_layer(blocks, w1)
    up[3], m = lax.optimization_barrier((up[3], m))
    last = lax.ppermute(up[3], "band", along_z(1))
    pieces = [own, up[1], down[1], up[2], down[2], up[3], down[3]]
    earlier = [0, -1, 1, -2, 2, -3, 3]
    before = decode_first(earlier, pieces, m, w2, head, small)
    fields = decode_last(earlier, [-4], [last], m, w2, head, small, before)
    return jnp.transpose(fields, (1, 0, 2))


def solution(mesh):
    return jax.shard_map(
        body,
        mesh=mesh,
        in_specs=(
            P("band", "patch", None),
            P(),
            P(),
            P("band", "patch", None),
            P("band", None, None),
            P("band", None),
            P("band", None, None),
            P("band", None),
            P("band", None),
            P("band", None, None),
            P("band", None),
        ),
        out_specs=P("band", None, "patch"),
        check_vma=False,
    )
```
